128 devices in a mesh: blk: 64 (over y, z, x_lo, core), rep: 2 (over x_hi).
Axes of the slice: x: 4 (x_hi: 2, x_lo: 2; x = x_hi * 2 + x_lo), y: 4, z: 4, core: 2. Of those that a mesh axis runs over, the one named last changes fastest.
Arguments:
- features: float32 [16384, 128], P('blk'), may hold values from -6 to 6
- weight: float32 [128, 256], replicated, may hold values from -0.5 to 0.5
- tile_values: float32 [64, 64, 3, 128, 128], P('blk'), may hold values from -0.0625 to 0.0625
- tile_pos: int32 [64, 64, 3], P('blk'), may hold values from 0 to 3, as said below
- tile_counts: int32 [64, 64], P('blk'), may hold values from 0 to 3, as said below
- out_grad: float32 [16384, 256], P('blk'), may hold values from -6 to 6
Outputs:
- output: float32 [16384, 256], P('blk')
- feature_grad: float32 [16384, 128], P('blk')
- weight_grad: float32 [128, 256], replicated
The draws below stay inside these ranges and needn't reach their ends.
Inputs may be any that keep to these rules, and one draw needn't show every extreme that they name: `tile_pos`: the 3 positions of one pair of blocks are different. `tile_counts`: every diagonal pair (b, b) holds 3 live tiles.
All inputs are finite; a program needn't handle non-finite values.
Results may differ from the reference program's by a relative error of at most 0.0003.
Values sent between devices are 32-bit elements; how exact they have to be, the bound alone decides.
A program may use at most 64 MiB of HBM per device.

```python
import math
import jax
import jax.numpy as jnp
from jax import lax

FIN = 128
D = 256
TILE = 128
NB = 256
MAXS = 3
TPB = 2
NODES = 16384
N_BLK = 64


def draw_tile_pos(key, part):
    key = jax.random.fold_in(key, 11)
    cells = TPB * TPB
    scores = jax.random.randint(key, (N_BLK, N_BLK, cells), 0, 1 << 20) * cells + jnp.arange(cells)
    ranked = jnp.argsort(scores, axis=-1)
    return ranked[..., :MAXS].astype(jnp.int32)


def draw_tile_counts(key, part):
    key = jax.random.fold_in(key, 23)
    level_key, count_key = jax.random.split(key)
    heavy_rows = jax.random.randint(level_key, (N_BLK, 1), 0, 4) == 0
    upper_bound = jnp.where(heavy_rows, MAXS + 1, 2)
    lower_bound = jnp.where(heavy_rows, 1, 0)
    counts = jax.random.randint(count_key, (N_BLK, N_BLK), lower_bound, upper_bound)
    diagonal = jnp.arange(N_BLK)[:, None] == jnp.arange(N_BLK)[None, :]
    return jnp.where(diagonal, MAXS, counts).astype(jnp.int32)


def steps_of(stream_key, extent, cuts, least, largest):
    gain, own = 1.0, jax.random.fold_in(stream_key, 6)
    for dim, shards_of in cuts:
        draws = jnp.exp(jax.random.uniform(jax.random.fold_in(own, dim), (shards_of,), jnp.float32, least / len(cuts), largest / len(cuts)))
        gain = gain * jnp.repeat(draws, extent[dim] // shards_of).reshape([-1 if axis == dim else 1 for axis in range(len(extent))])
    return gain


def bell_draw(rng, extent, width, bound, pieces=(), kind=jnp.bfloat16):
    drawn = width * jax.random.normal(rng, extent, jnp.float32)
    if pieces:
        drawn = drawn * steps_of(rng, extent, pieces, -0.22, 0.18)
    return jnp.clip(drawn, -bound, bound).astype(kind)


def setup_inputs(seed: int = 0) -> dict:
    key_of = jax.random.split(jax.random.key(seed), 7)
    return {
        "features": bell_draw(key_of[0], (NODES, FIN), 1.0, 6.0, ((0, 64),), jnp.float32),
        "weight": bell_draw(key_of[1], (FIN, D), FIN ** -0.5, 0.5, (), jnp.float32),
        "tile_values": bell_draw(key_of[2], (N_BLK, N_BLK, MAXS, TILE, TILE), (N_BLK * TILE) ** -0.5, 0.0625, ((0, 64),), jnp.float32),
        "tile_pos": draw_tile_pos(jax.random.fold_in(key_of[6], 71), 0),
        "tile_counts": draw_tile_counts(jax.random.fold_in(key_of[6], 71), 0),
        "out_grad": bell_draw(key_of[5], (NODES, D), 1.0, 6.0, ((0, 64),), jnp.float32),
    }


HIGHEST = lax.Precision.HIGHEST

def aggregate(features, tile_values, tile_pos, tile_counts):
    feature_width = features.shape[1]
    tile_grid = features.reshape(N_BLK, TPB, TILE, feature_width)

    def one_block(pair_items):
        values, positions, live_count = pair_items
        picked = tile_grid[jnp.arange(N_BLK)[:, None], positions % TPB]
        active = (jnp.arange(MAXS)[None, :] < live_count[:, None]).astype(jnp.float32)
        product = jnp.einsum('csij,csjf->csif', values, picked, precision=HIGHEST)
        placing = (positions[..., None] // TPB == jnp.arange(TPB)).astype(jnp.float32) * active[..., None]
        return jnp.einsum('cst,csif->tif', placing, product, precision=HIGHEST).reshape(NB, feature_width)
    blocks_out = lax.map(one_block, (tile_values, tile_pos, tile_counts))
    return blocks_out.reshape(NODES, feature_width)

def spread_back(agg_grad, tile_values, tile_pos, tile_counts):
    feature_width = agg_grad.shape[1]
    block_grads = agg_grad.reshape(N_BLK, TPB, TILE, feature_width)

    def absorb(running_sum, pair_items):
        values, positions, live_count, block_grad = pair_items
        picked = block_grad[positions // TPB]
        active = (jnp.arange(MAXS)[None, :] < live_count[:, None]).astype(jnp.float32)
        product = jnp.einsum('csij,csif->csjf', values, picked, precision=HIGHEST)
        placing = (positions[..., None] % TPB == jnp.arange(TPB)).astype(jnp.float32) * active[..., None]
        return (running_sum + jnp.einsum('cst,csjf->ctjf', placing, product, precision=HIGHEST), None)
    start_sum = jnp.zeros((N_BLK, TPB, TILE, feature_width), jnp.float32)
    result, ignored = lax.scan(absorb, start_sum, (tile_values, tile_pos, tile_counts, block_grads))
    return result.reshape(NODES, feature_width)

def reference(features, weight, tile_values, tile_pos, tile_counts, out_grad):
    aggregated = aggregate(features, tile_values, tile_pos, tile_counts)
    pre_act = jnp.dot(aggregated, weight, precision=HIGHEST)
    gate_value = jax.nn.sigmoid(pre_act)
    output = pre_act * gate_value
    pre_grad = out_grad * gate_value * (1.0 + pre_act * (1.0 - gate_value))
    weight_grad = jnp.einsum('nf,nd->fd', aggregated, pre_grad, precision=HIGHEST) / math.sqrt(NODES)
    agg_grad = jnp.dot(pre_grad, weight.T, precision=HIGHEST)
    feature_grad = spread_back(agg_grad, tile_values, tile_pos, tile_counts)
    return (output, feature_grad, weight_grad)
```

```python
import math

import jax
import jax.numpy as jnp
from jax import lax
from jax.experimental import pallas as pl
from jax.experimental.pallas import tpu as pltpu
from jax.sharding import PartitionSpec as P

HIGHEST = lax.Precision.HIGHEST
MESH = pl.DeviceIdType.MESH
F32, BF16 = jnp.float32, jnp.bfloat16
NODES = 16384
TILE = 128


def split(x):
    hi = x.astype(BF16)
    return hi, (x - hi.astype(F32)).astype(BF16)


def kernel(
    feat_hbm, weight_hbm, tiles_hbm, pos, counts, ograd_hbm,
    out_hbm, fgrad_hbm, wgrad_hbm,
    tv, ah, al, feat, wside, acc, swap, agg_t, wt, og, pgrad, gs, outv,
    part, sibq, b_opp, b_full, a_opp, a_full, xr, fgv,
    wg, wr1, wr2, fin, wr3, wgv,
    tile_sem, load_sem, first_sem, store_sem,
    f_send, f_recv, fs_send, fs_recv, x_send, x_recv, swap_send, swap_recv,
    q_send, q_recv, bo_send, bo_recv, bf_send, bf_recv, ao_send, ao_recv, af_send, af_recv,
    t_send, t_recv, w1_send, w1_recv, w2_send, w2_recv, w3_send, w3_recv,
):
    blk, rep = lax.axis_index("blk"), lax.axis_index("rep")
    y, z = lax.rem(lax.div(blk, 16), 4), lax.rem(lax.div(blk, 4), 4)
    xl, k = lax.rem(lax.div(blk, 2), 2), lax.rem(blk, 2)
    native = xl == rep

    def at(yy, zz, xx, kk):
        return ((lax.rem(yy + 8, 4) * 4 + lax.rem(zz + 8, 4)) * 2 + xx) * 2 + kk

    def near(da, db):
        return (at(y + da * (1 - k) + db * k, z + da * k + db * (1 - k), xl, k), rep)

    sibling = (at(y, z, xl, 1 - k), rep)

    def remote(src, dst, ssem, rsem, dev):
        return pltpu.make_async_remote_copy(
            src_ref=src, dst_ref=dst, send_sem=ssem, recv_sem=rsem, device_id=dev, device_id_type=MESH
        )

    def arrived(dst, rsem):
        remote(dst, dst, rsem, rsem, sibling).wait_recv()

    def sent(src, ssem):
        remote(src, src, ssem, ssem, sibling).wait_send()

    tile_copy = pltpu.make_async_copy(tiles_hbm.at[:, rep], tv, tile_sem)
    tile_copy.start()
    loads = [
        pltpu.make_async_copy(weight_hbm, wt, load_sem.at[0]),
        pltpu.make_async_copy(ograd_hbm, og, load_sem.at[1]),
    ]
    for c in loads:
        c.start()

    barrier = pltpu.get_barrier_semaphore()
    plane_peers = [(dy, dz) for dy in range(4) for dz in range(4) if (dy, dz) != (0, 0)]
    line_peers = [(i, j, l) for i in range(2) for j in range(2) for l in range(2) if (i, j, l) != (0, 0, 0)]

    def plane_dev(dy, dz):
        return (at(y + dy, z + dz, xl, k), rep)

    def line_dev(i, j, l):
        return (at(y, z, lax.rem(xl + j, 2), lax.rem(k + l, 2)), lax.rem(rep + i, 2))

    for d in plane_peers:
        pl.semaphore_signal(barrier, inc=1, device_id=plane_dev(*d), device_id_type=MESH)
    for d in line_peers:
        pl.semaphore_signal(barrier, inc=1, device_id=line_dev(*d), device_id_type=MESH)
    pl.semaphore_wait(barrier, len(plane_peers) + len(line_peers))

    half = lax.rem(xl + rep, 2)
    remote(
        feat_hbm.at[half], feat.at[0, half], x_send, x_recv.at[half], (at(y, z, 1 - xl, k), xl)
    ).start()

    @pl.when(native)
    def _():
        c = pltpu.make_async_copy(feat_hbm, feat.at[0, pl.ds(0, 2)], first_sem)
        c.start()
        c.wait()

    @pl.when(jnp.logical_not(native))
    def _():
        for h in range(2):
            arrived(feat.at[0, h], x_recv.at[h])

    def spot(da, db, h):
        return (da % 4 * 4 + db % 4) * 2 + h

    def send_f(da, db, h, ma, mb):
        there = spot(da - ma, db - mb, h)
        remote(
            feat.at[0, spot(da, db, h)], feat.at[0, there], f_send, f_recv.at[there], near(ma, mb)
        ).start()

    def wait_f(da, db, h):
        i = spot(da, db, h)
        arrived(feat.at[0, i], f_recv.at[i])

    def give_f(da, db):
        i = spot(da, db, 0)
        remote(
            feat.at[0, pl.ds(i, 2)], feat.at[1, pl.ds(i, 2)], fs_send, fs_recv.at[i // 2], sibling
        ).start()

    def prep(kk, da):
        def one(db, carry):
            if kk == 0:
                own = k
            else:
                own = 1 - k
            yy = lax.rem(y + da * (1 - own) + db * own, 4)
            zz = lax.rem(z + da * own + db * (1 - own), 4)
            c = ((yy * 4 + zz) * 2 + rep) * 2 + own
            base = yy * 4 + zz
            n = counts[0, c]
            p = [pos[0, c, s] for s in range(3)]
            for q in range(4):
                s = jnp.where(p[0] == q, 0, jnp.where(p[1] == q, 1, 2))
                live = ((p[0] == q) & (n > 0)) | ((p[1] == q) & (n > 1)) | ((p[2] == q) & (n > 2))
                t = tv[base, own, s] * jnp.where(live, 1.0, 0.0).astype(F32)
                hi, lo = split(t)
                col = pl.multiple_of((kk * 16 + da * 4 + db) * 256 + q % 2 * TILE, TILE)
                rows = slice(q // 2 * TILE, (q // 2 + 1) * TILE)
                ah[rows, pl.ds(col, TILE)] = hi
                al[rows, pl.ds(col, TILE)] = lo
            return carry

        lax.fori_loop(0, 4, one, 0)

    def multiply(kk, da):
        hi, lo = split(feat[kk, da * 8 : da * 8 + 8].reshape(1024, TILE))
        wside[:, 0:TILE] = hi
        wside[:, TILE : 2 * TILE] = lo
        cols = slice((kk * 16 + da * 4) * 256, (kk * 16 + da * 4 + 4) * 256)
        w = wside[...]
        acc[...] += jnp.dot(ah[:, cols], w, preferred_element_type=F32) + jnp.dot(
            al[:, cols], w, preferred_element_type=F32
        )

    def sib_group(da):
        for db in range(4):
            i = da * 4 + db
            arrived(feat.at[1, pl.ds(2 * i, 2)], fs_recv.at[i])

    for h in range(2):
        send_f(0, 0, h, 1, 0)
        send_f(0, 0, 1 - h, -1, 0)
    for h in range(2):
        send_f(0, 0, h, 0, 1)
        send_f(0, 0, 1 - h, 0, -1)
    give_f(0, 0)
    acc[...] = jnp.zeros_like(acc)
    tile_copy.wait()
    prep(0, 0)
    wait_f(3, 0, 0)
    send_f(3, 0, 0, 1, 0)
    wait_f(1, 0, 1)
    send_f(1, 0, 1, -1, 0)
    wait_f(3, 0, 1)
    wait_f(1, 0, 0)
    for da in (3, 1):
        give_f(da, 0)
    for h in range(2):
        for da in (3, 1):
            send_f(da, 0, h, 0, 1)
            send_f(da, 0, 1 - h, 0, -1)
    prep(1, 0)
    wait_f(0, 3, 0)
    send_f(0, 3, 0, 0, 1)
    wait_f(0, 1, 1)
    send_f(0, 1, 1, 0, -1)
    wait_f(2, 0, 0)
    wait_f(2, 0, 1)
    give_f(2, 0)
    for h in range(2):
        send_f(2, 0, h, 0, 1)
        send_f(2, 0, 1 - h, 0, -1)
    wait_f(0, 3, 1)
    give_f(0, 3)
    wait_f(0, 1, 0)
    give_f(0, 1)
    prep(0, 3)
    for da in (3, 1, 2):
        wait_f(da, 3, 0)
        send_f(da, 3, 0, 0, 1)
        wait_f(da, 1, 1)
        send_f(da, 1, 1, 0, -1)
        wait_f(da, 3, 1)
        give_f(da, 3)
        wait_f(da, 1, 0)
        give_f(da, 1)
        before = {3: 0, 1: 3, 2: 1}[da]
        wait_f(before, 2, 0)
        wait_f(before, 2, 1)
        give_f(before, 2)
        if da == 3:
            prep(1, 3)
            prep(0, 1)
        if da == 1:
            prep(1, 1)
            prep(0, 2)
            prep(1, 2)
        multiply(0, before)
        sib_group(before)
        multiply(1, before)
    wait_f(2, 2, 0)
    wait_f(2, 2, 1)
    give_f(2, 2)
    multiply(0, 2)
    sib_group(2)
    multiply(1, 2)

    swap[0] = acc[:, 0:TILE] + acc[:, TILE : 2 * TILE]
    twin = (blk, 1 - rep)
    c = remote(swap.at[0], swap.at[1], swap_send, swap_recv, twin)
    c.start()
    for l in loads:
        l.wait()
    c.wait_recv()
    agg = swap[0] + swap[1]
    w = wt[...]
    pre = jnp.dot(agg, w, precision=HIGHEST, preferred_element_type=F32)
    gate = jax.nn.sigmoid(pre)
    outv[...] = pre * gate
    pg = og[...] * gate * (1.0 + pre * (1.0 - gate))
    pgrad[...] = pg
    g_t = lax.dot_general(w, pg, (((1,), (1,)), ((), ())), precision=HIGHEST, preferred_element_type=F32)
    hi, lo = split(g_t)
    gs[0:TILE] = hi
    gs[TILE : 2 * TILE] = lo
    out_copy = pltpu.make_async_copy(outv, out_hbm, store_sem.at[0])
    out_copy.start()

    def back(kk, da):
        cols = slice((kk * 16 + da * 4) * 256, (kk * 16 + da * 4 + 4) * 256)
        main = jnp.dot(gs[...], ah[:, cols], preferred_element_type=F32)
        rest = jnp.dot(gs[0:TILE], al[:, cols], preferred_element_type=F32)
        total = main[0:TILE] + main[TILE : 2 * TILE] + rest
        for db in range(4):
            for h in range(2):
                part[kk, spot(da, db, h)] = total[h * 64 : h * 64 + 64, db * 256 : db * 256 + 256]

    def give_q(da):
        for db in (2, 1, 3, 0):
            i = spot(da, db, 0)
            remote(
                part.at[1, pl.ds(i, 2)], sibq.at[pl.ds(i, 2)], q_send, q_recv.at[i // 2], sibling
            ).start()

    def take_q(da, db):
        i = spot(da, db, 0)
        arrived(sibq.at[pl.ds(i, 2)], q_recv.at[i // 2])
        part[0, i : i + 2] = part[0, i : i + 2] + sibq[i : i + 2]

    def step1(da):
        take_q(da, 2)
        for h, m in ((0, 1), (1, -1)):
            remote(
                part.at[0, spot(da, 2, h)], b_opp.at[da, h], bo_send, bo_recv.at[da, h], near(0, m)
            ).start()

    def send_full(da, db, h, n, m):
        remote(
            part.at[0, spot(da, db, h)], b_full.at[da, n, h], bf_send, bf_recv.at[da, n, h], near(0, m)
        ).start()

    def step2(da):
        take_q(da, 1)
        send_full(da, 1, 1, 0, 1)
        take_q(da, 3)
        send_full(da, 3, 0, 1, -1)
        for db, h, m in ((1, 0, 1), (3, 1, -1)):
            arrived(b_opp.at[da, h], bo_recv.at[da, h])
            i = spot(da, db, h)
            part[0, i] = part[0, i] + b_opp[da, h]
            send_full(da, db, h, h, m)

    def step3(da):
        take_q(da, 0)
        for n in range(2):
            for h in range(2):
                arrived(b_full.at[da, n, h], bf_recv.at[da, n, h])
        i = spot(da, 0, 0)
        part[0, i : i + 2] = part[0, i : i + 2] + (b_full[da, 0] + b_full[da, 1])

    def send_a(da, h, n, m):
        remote(
            part.at[0, spot(da, 0, h)], a_full.at[n, h], af_send, af_recv.at[n, h], near(m, 0)
        ).start()

    def weight_term():
        agg_t[...] = (swap[0] + swap[1]).T
        rows = agg_t[pl.ds(pl.multiple_of(rep * 64, 64), 64), :]
        term = jnp.dot(rows, pgrad[...], precision=HIGHEST, preferred_element_type=F32)
        for i in range(8):
            for j in range(2):
                wg[i * 2 + j] = term[i * 8 : i * 8 + 8, j * TILE : j * TILE + TILE]
        for dy, dz in plane_peers:
            there = lax.rem(y + dy, 4) * 4 + lax.rem(z + dz, 4)
            remote(wg.at[there], wr1.at[dy * 4 + dz - 1], w1_send, w1_recv, plane_dev(dy, dz)).start()

    here = y * 4 + z
    line = (rep * 2 + xl) * 2 + k

    def weight_line():
        arrived(wr1, w1_recv)
        total = wg[here]
        for i in range(15):
            total = total + wr1[i]
        wr2[line] = total
        for d in line_peers:
            remote(wr2.at[line], wr2.at[line], w2_send, w2_recv, line_dev(*d)).start()

    def weight_plane():
        arrived(wr2.at[pl.ds(0, 7)], w2_recv)
        for i in range(2):
            total = (wr2[4 * i] + wr2[4 * i + 1]) + (wr2[4 * i + 2] + wr2[4 * i + 3])
            wr3[here, i] = total * (1.0 / math.sqrt(NODES))
        for d in plane_peers:
            remote(wr3.at[here], wr3.at[here], w3_send, w3_recv, plane_dev(*d)).start()

    back(1, 2)
    give_q(2)
    back(0, 2)
    step1(2)
    back(1, 1)
    give_q(1)
    step2(2)
    back(0, 1)
    step1(1)
    back(1, 3)
    give_q(3)
    step2(1)
    back(0, 3)
    step1(3)
    back(1, 0)
    give_q(0)
    step2(3)
    back(0, 0)
    step1(0)
    step2(0)
    weight_term()
    step3(2)
    for h, m in ((0, 1), (1, -1)):
        remote(part.at[0, spot(2, 0, h)], a_opp.at[h], ao_send, ao_recv.at[h], near(m, 0)).start()
    step3(1)
    send_a(1, 1, 0, 1)
    weight_line()
    step3(3)
    send_a(3, 0, 1, -1)
    for da, h, m in ((1, 0, 1), (3, 1, -1)):
        arrived(a_opp.at[h], ao_recv.at[h])
        i = spot(da, 0, h)
        part[0, i] = part[0, i] + a_opp[h]
        send_a(da, h, h, m)
    weight_plane()
    step3(0)
    for n in range(2):
        for h in range(2):
            arrived(a_full.at[n, h], af_recv.at[n, h])
    part[0, 0:2] = part[0, 0:2] + (a_full[0] + a_full[1])

    total = part.at[0, pl.ds(0, 2)]

    @pl.when(native)
    def _():
        remote(total, xr.at[1], t_send.at[0], t_recv.at[1], (at(y, z, xl, k), 1 - rep)).start()
        arrived(xr.at[0], t_recv.at[0])
        fgv[...] = (part[0, 0:2] + xr[0]).reshape(TILE, 256).T
        sent(total, t_send.at[0])

    @pl.when(jnp.logical_not(native))
    def _():
        remote(total, xr.at[0], t_send.at[0], t_recv.at[0], (at(y, z, 1 - xl, k), rep)).start()
        remote(total, xr.at[0], t_send.at[1], t_recv.at[0], (at(y, z, 1 - xl, k), 1 - rep)).start()
        arrived(xr.at[0], t_recv.at[0])
        arrived(xr.at[1], t_recv.at[1])
        fgv[...] = (xr[0] + xr[1]).reshape(TILE, 256).T
        sent(total, t_send.at[0])
        sent(total, t_send.at[1])

    fg_copy = pltpu.make_async_copy(fgv, fgrad_hbm, store_sem.at[1])
    fg_copy.start()

    arrived(wr3.at[pl.ds(0, 15)], w3_recv)
    for half_index in range(2):
        for i in range(8):
            for j in range(2):
                wgv[half_index * 64 + i * 8 : half_index * 64 + i * 8 + 8, j * TILE : j * TILE + TILE] = wr3[
                    i * 2 + j, half_index
                ]
    wg_copy = pltpu.make_async_copy(wgv, wgrad_hbm, store_sem.at[2])
    wg_copy.start()

    sent(feat.at[0, half], x_send)
    sent(feat.at[0, pl.ds(0, 30)], f_send)
    sent(feat.at[0], fs_send)
    sent(swap.at[0], swap_send)
    sent(part.at[1], q_send)
    sent(b_opp, bo_send)
    sent(b_full, bf_send)
    sent(a_opp, ao_send)
    sent(a_full, af_send)
    sent(wr1, w1_send)
    sent(wr2.at[pl.ds(0, 7)], w2_send)
    sent(wr3.at[pl.ds(0, 15)], w3_send)
    out_copy.wait()
    fg_copy.wait()
    wg_copy.wait()


def body(features, weight, tile_values, tile_pos, tile_counts, out_grad):
    dma = pltpu.SemaphoreType.DMA
    vm = pltpu.VMEM
    any_space = pl.BlockSpec(memory_space=pl.ANY)
    smem = pl.BlockSpec(memory_space=pltpu.SMEM)
    return pl.pallas_call(
        kernel,
        out_shape=(
            jax.ShapeDtypeStruct((256, 256), F32),
            jax.ShapeDtypeStruct((256, 128), F32),
            jax.ShapeDtypeStruct((128, 256), F32),
        ),
        in_specs=[any_space, any_space, any_space, smem, smem, any_space],
        out_specs=(any_space, any_space, any_space),
        scratch_shapes=[
            vm((16, 2, 3, TILE, TILE), F32),
            vm((256, 8192), BF16),
            vm((256, 8192), BF16),
            vm((2, 32, TILE, TILE), F32),
            vm((1024, 256), BF16),
            vm((256, 256), F32),
            vm((2, 256, TILE), F32),
            vm((TILE, 256), F32),
            vm((TILE, 256), F32),
            vm((256, 256), F32),
            vm((256, 256), F32),
            vm((256, 256), BF16),
            vm((256, 256), F32),
            vm((2, 32, 64, 256), F32),
            vm((32, 64, 256), F32),
            vm((4, 2, 64, 256), F32),
            vm((4, 2, 2, 64, 256), F32),
            vm((2, 64, 256), F32),
            vm((2, 2, 64, 256), F32),
            vm((2, 2, 64, 256), F32),
            vm((256, TILE), F32),
            vm((16, 8, TILE), F32),
            vm((15, 8, TILE), F32),
            vm((8, 8, TILE), F32),
            vm((8, TILE), F32),
            vm((16, 2, 8, TILE), F32),
            vm((TILE, 256), F32),
            dma, dma((2,)), dma, dma((3,)),
            dma, dma((32,)), dma, dma((16,)), dma, dma((2,)), dma, dma,
            dma, dma((16,)), dma, dma((4, 2)), dma, dma((4, 2, 2)), dma, dma((2,)), dma, dma((2, 2)),
            dma((2,)), dma((2,)), dma, dma, dma, dma, dma, dma,
        ],
        compiler_params=pltpu.CompilerParams(
            collective_id=0, has_side_effects=True, vmem_limit_bytes=48 * 1024 * 1024
        ),
        cost_estimate=pl.CostEstimate(flops=3_000_000_000, bytes_accessed=8_000_000, transcendentals=65536),
    )(
        features.reshape(2, TILE, TILE),
        weight,
        tile_values.reshape(16, 2, 2, 3, TILE, TILE),
        tile_pos,
        tile_counts,
        out_grad,
    )


def solution(mesh):
    return jax.shard_map(
        body,
        mesh=mesh,
        in_specs=(
            P("blk", None),
            P(),
            P("blk", None, None, None, None),
            P("blk", None, None),
            P("blk", None),
            P("blk", None),
        ),
        out_specs=(P("blk", None), P("blk", None), P()),
        check_vma=False,
    )
```

```python
import math

import jax
import jax.numpy as jnp
from jax import lax
from jax.experimental import pallas as pl
from jax.experimental.pallas import tpu as pltpu
from jax.sharding import PartitionSpec as P

HIGHEST = lax.Precision.HIGHEST
MESH = pl.DeviceIdType.MESH
F32, BF16 = jnp.float32, jnp.bfloat16
NODES = 16384
TILE = 128


def split(x):
    hi = x.astype(BF16)
    return hi, (x - hi.astype(F32)).astype(BF16)


def kernel(
    feat_hbm, weight_hbm, tiles_hbm, pos, counts, ograd_hbm,
    out_hbm, fgrad_hbm, wgrad_hbm,
    tv, ah, al, feat, wside, acc, swap, agg_t, wt, og, pgrad, gs, outv,
    part, sibq, b_opp, b_full, a_full, xr, fgv,
    wg, wr1, wr2, wr3, wgv,
    tile_sem, load_sem, first_sem, store_sem,
    f_send, f_recv, fs_send, fs_recv, x_send, n_send, swap_send, swap_recv,
    q_send, q_recv, bo_send, bo_recv, bf_send, bf_recv, af_send, af_recv,
    t_send, t_recv, w1_send, w1_recv, w2_send, w2_recv, w3_send, w3_recv,
):
    blk, rep = lax.axis_index("blk"), lax.axis_index("rep")
    y, z = lax.rem(lax.div(blk, 16), 4), lax.rem(lax.div(blk, 4), 4)
    xl, k = lax.rem(lax.div(blk, 2), 2), lax.rem(blk, 2)
    native = k == rep

    def at(yy, zz, xx, kk):
        return ((lax.rem(yy + 8, 4) * 4 + lax.rem(zz + 8, 4)) * 2 + xx) * 2 + kk

    def near(da, db):
        return (at(y + da * (1 - k) + db * k, z + da * k + db * (1 - k), xl, k), rep)

    sibling = (at(y, z, xl, 1 - k), rep)

    def remote(src, dst, ssem, rsem, dev):
        return pltpu.make_async_remote_copy(
            src_ref=src, dst_ref=dst, send_sem=ssem, recv_sem=rsem, device_id=dev, device_id_type=MESH
        )

    def arrived(dst, rsem):
        remote(dst, dst, rsem, rsem, sibling).wait_recv()

    def sent(src, ssem):
        remote(src, src, ssem, ssem, sibling).wait_send()

    tile_copy = pltpu.make_async_copy(tiles_hbm.at[:, :, rep], tv, tile_sem)
    tile_copy.start()
    loads = [
        pltpu.make_async_copy(weight_hbm, wt, load_sem.at[0]),
        pltpu.make_async_copy(ograd_hbm, og, load_sem.at[1]),
    ]
    for c in loads:
        c.start()

    barrier = pltpu.get_barrier_semaphore()
    plane_peers = [(dy, dz) for dy in range(4) for dz in range(4) if (dy, dz) != (0, 0)]
    line_peers = [(i, j, l) for i in range(2) for j in range(2) for l in range(2) if (i, j, l) != (0, 0, 0)]

    def plane_dev(dy, dz):
        return (at(y + dy, z + dz, xl, k), rep)

    def line_dev(i, j, l):
        return (at(y, z, lax.rem(xl + j, 2), lax.rem(k + l, 2)), lax.rem(rep + i, 2))

    def over(m):
        return (at(y + m * k, z + m * (1 - k), 1 - xl, 1 - k), k)

    def over_from(m, i):
        return (at(y + m * (1 - k), z + m * k, 1 - xl, 1 - k), i)

    def greet(dev):
        pl.semaphore_signal(barrier, inc=1, device_id=dev, device_id_type=MESH)

    twin = (blk, 1 - rep)
    peers = [near(1, 0), near(-1, 0), near(2, 0), near(0, 1), near(0, -1), sibling, twin]
    for d in peers:
        greet(d)

    for i in range(2):
        greet((at(y, z, 1 - xl, 1 - k), i))

    @pl.when(jnp.logical_not(native))
    def _():
        for m in (1, -1, 2):
            for i in range(2):
                greet(over_from(m, i))

    pl.semaphore_wait(barrier, len(peers) + 2 + 3)

    def spot(da, db, h):
        return (da % 4 * 4 + db % 4) * 2 + h

    def send_f(da, db, h, ma, mb):
        there = spot(da - ma, db - mb, h)
        remote(
            feat.at[0, spot(da, db, h)], feat.at[0, there], f_send, f_recv.at[there], near(ma, mb)
        ).start()

    def wait_f(da, db, h):
        i = spot(da, db, h)
        arrived(feat.at[0, i], f_recv.at[i])

    def give_f(da, db):
        i = spot(da, db, 0)
        remote(
            feat.at[0, pl.ds(i, 2)], feat.at[1, pl.ds(i, 2)], fs_send, fs_recv.at[i // 2], sibling
        ).start()

    def prep(kk, da):
        def one(db, carry):
            if kk == 0:
                own = k
            else:
                own = 1 - k
            yy = lax.rem(y + da * (1 - own) + db * own, 4)
            zz = lax.rem(z + da * own + db * (1 - own), 4)
            xx = lax.rem(xl + own + rep, 2)
            base = yy * 4 + zz
            c = (base * 2 + xx) * 2 + rep
            n = counts[0, c]
            p = [pos[s, 0, c] for s in range(3)]
            for q in range(4):
                s = jnp.where(p[0] == q, 0, jnp.where(p[1] == q, 1, 2))
                live = ((p[0] == q) & (n > 0)) | ((p[1] == q) & (n > 1)) | ((p[2] == q) & (n > 2))
                t = tv[base, xx, s] * jnp.where(live, 1.0, 0.0).astype(F32)
                hi, lo = split(t)
                col = pl.multiple_of((kk * 16 + da * 4 + db) * 256 + q % 2 * TILE, TILE)
                rows = slice(q // 2 * TILE, (q // 2 + 1) * TILE)
                ah[rows, pl.ds(col, TILE)] = hi
                al[rows, pl.ds(col, TILE)] = lo
            return carry

        lax.fori_loop(0, 4, one, 0)

    def multiply(kk, da):
        hi, lo = split(feat[kk, da * 8 : da * 8 + 8].reshape(1024, TILE))
        wside[:, 0:TILE] = hi
        wside[:, TILE : 2 * TILE] = lo
        cols = slice((kk * 16 + da * 4) * 256, (kk * 16 + da * 4 + 4) * 256)
        w = wside[...]
        acc[...] += jnp.dot(ah[:, cols], w, preferred_element_type=F32) + jnp.dot(
            al[:, cols], w, preferred_element_type=F32
        )

    def sib_group(da):
        for db in range(4):
            i = da * 4 + db
            arrived(feat.at[1, pl.ds(2 * i, 2)], fs_recv.at[i])

    half = lax.rem(k + rep, 2)
    for m in (0, 1, -1, 2):
        i = spot(-m, 0, 0) + half
        remote(feat_hbm.at[half], feat.at[0, i], x_send, f_recv.at[i], over(m)).start()
    first_copy = pltpu.make_async_copy(feat_hbm, feat.at[0, pl.ds(0, 2)], first_sem)

    @pl.when(native)
    def _():
        first_copy.start()
        for m in (1, -1, 2):
            for h in range(2):
                i = spot(-m, 0, h)
                remote(feat_hbm.at[h], feat.at[0, i], n_send, f_recv.at[i], near(m, 0)).start()
        first_copy.wait()

    @pl.when(jnp.logical_not(native))
    def _():
        for h in range(2):
            wait_f(0, 0, h)

    for h in range(2):
        send_f(0, 0, h, 0, 1)
        send_f(0, 0, 1 - h, 0, -1)
    give_f(0, 0)
    acc[...] = jnp.zeros_like(acc)
    tile_copy.wait()
    prep(0, 0)
    for da in (3, 1):
        for h in range(2):
            wait_f(da, 0, h)
        give_f(da, 0)
        for h in range(2):
            send_f(da, 0, h, 0, 1)
            send_f(da, 0, 1 - h, 0, -1)
    prep(1, 0)
    wait_f(0, 3, 0)
    send_f(0, 3, 0, 0, 1)
    wait_f(0, 1, 1)
    send_f(0, 1, 1, 0, -1)
    wait_f(2, 0, 0)
    wait_f(2, 0, 1)
    give_f(2, 0)
    for h in range(2):
        send_f(2, 0, h, 0, 1)
        send_f(2, 0, 1 - h, 0, -1)
    wait_f(0, 3, 1)
    give_f(0, 3)
    wait_f(0, 1, 0)
    give_f(0, 1)
    prep(0, 3)
    for da in (3, 1, 2):
        wait_f(da, 3, 0)
        send_f(da, 3, 0, 0, 1)
        wait_f(da, 1, 1)
        send_f(da, 1, 1, 0, -1)
        wait_f(da, 3, 1)
        give_f(da, 3)
        wait_f(da, 1, 0)
        give_f(da, 1)
        before = {3: 0, 1: 3, 2: 1}[da]
        wait_f(before, 2, 0)
        wait_f(before, 2, 1)
        give_f(before, 2)
        if da == 3:
            prep(1, 3)
            prep(0, 1)
        if da == 1:
            prep(1, 1)
            prep(0, 2)
            prep(1, 2)
        multiply(0, before)
        sib_group(before)
        multiply(1, before)
    wait_f(2, 2, 0)
    wait_f(2, 2, 1)
    give_f(2, 2)
    multiply(0, 2)
    sib_group(2)
    multiply(1, 2)

    swap[0] = acc[:, 0:TILE] + acc[:, TILE : 2 * TILE]
    c = remote(swap.at[0], swap.at[1], swap_send, swap_recv, twin)
    c.start()
    for l in loads:
        l.wait()
    c.wait_recv()
    agg = swap[0] + swap[1]
    w = wt[...]
    pre = jnp.dot(agg, w, precision=HIGHEST, preferred_element_type=F32)
    gate = jax.nn.sigmoid(pre)
    outv[...] = pre * gate
    pg = og[...] * gate * (1.0 + pre * (1.0 - gate))
    pgrad[...] = pg
    g_t = lax.dot_general(w, pg, (((1,), (1,)), ((), ())), precision=HIGHEST, preferred_element_type=F32)
    hi, lo = split(g_t)
    gs[0:TILE] = hi
    gs[TILE : 2 * TILE] = lo
    out_copy = pltpu.make_async_copy(outv, out_hbm, store_sem.at[0])
    out_copy.start()

    def back(kk, da):
        cols = slice((kk * 16 + da * 4) * 256, (kk * 16 + da * 4 + 4) * 256)
        main = jnp.dot(gs[...], ah[:, cols], preferred_element_type=F32)
        rest = jnp.dot(gs[0:TILE], al[:, cols], preferred_element_type=F32)
        total = main[0:TILE] + main[TILE : 2 * TILE] + rest
        for db in range(4):
            for h in range(2):
                part[kk, spot(da, db, h)] = total[h * 64 : h * 64 + 64, db * 256 : db * 256 + 256]

    def give_q(da):
        for db in (2, 1, 3, 0):
            i = spot(da, db, 0)
            remote(
                part.at[1, pl.ds(i, 2)], sibq.at[pl.ds(i, 2)], q_send, q_recv.at[i // 2], sibling
            ).start()

    def take_q(da, db):
        i = spot(da, db, 0)
        arrived(sibq.at[pl.ds(i, 2)], q_recv.at[i // 2])
        part[0, i : i + 2] = part[0, i : i + 2] + sibq[i : i + 2]

    def step1(da):
        take_q(da, 2)
        for h, m in ((0, 1), (1, -1)):
            remote(
                part.at[0, spot(da, 2, h)], b_opp.at[da, h], bo_send, bo_recv.at[da, h], near(0, m)
            ).start()

    def send_full(da, db, h, n, m):
        remote(
            part.at[0, spot(da, db, h)], b_full.at[da, n, h], bf_send, bf_recv.at[da, n, h], near(0, m)
        ).start()

    def step2(da):
        take_q(da, 1)
        send_full(da, 1, 1, 0, 1)
        take_q(da, 3)
        send_full(da, 3, 0, 1, -1)

    def step2_sums(da):
        for db, h, m in ((1, 0, 1), (3, 1, -1)):
            arrived(b_opp.at[da, h], bo_recv.at[da, h])
            i = spot(da, db, h)
            part[0, i] = part[0, i] + b_opp[da, h]
            send_full(da, db, h, h, m)

    def step3(da):
        take_q(da, 0)
        for n in range(2):
            for h in range(2):
                arrived(b_full.at[da, n, h], bf_recv.at[da, n, h])
        i = spot(da, 0, 0)
        part[0, i : i + 2] = part[0, i : i + 2] + (b_full[da, 0] + b_full[da, 1])

    def send_a(da, n, m):
        i = spot(da, 0, 0)
        remote(part.at[0, pl.ds(i, 2)], a_full.at[n], af_send, af_recv.at[n], near(m, 0)).start()

    def weight_term():
        agg_t[...] = (swap[0] + swap[1]).T
        rows = agg_t[pl.ds(pl.multiple_of(rep * 64, 64), 64), :]
        term = jnp.dot(rows, pgrad[...], precision=HIGHEST, preferred_element_type=F32)
        for i in range(8):
            for j in range(2):
                wg[i * 2 + j] = term[i * 8 : i * 8 + 8, j * TILE : j * TILE + TILE]
        for dy, dz in plane_peers:
            there = lax.rem(y + dy, 4) * 4 + lax.rem(z + dz, 4)
            remote(wg.at[there], wr1.at[dy * 4 + dz - 1], w1_send, w1_recv, plane_dev(dy, dz)).start()

    here = y * 4 + z
    line = (rep * 2 + xl) * 2 + k

    def weight_line():
        arrived(wr1, w1_recv)
        total = wg[here]
        for i in range(15):
            total = total + wr1[i]
        wr2[line] = total
        for d in line_peers:
            remote(wr2.at[line], wr2.at[line], w2_send, w2_recv, line_dev(*d)).start()

    def weight_plane():
        arrived(wr2.at[pl.ds(0, 7)], w2_recv)
        for i in range(2):
            total = (wr2[4 * i] + wr2[4 * i + 1]) + (wr2[4 * i + 2] + wr2[4 * i + 3])
            wr3[here, i] = total * (1.0 / math.sqrt(NODES))
        for d in plane_peers:
            remote(wr3.at[here], wr3.at[here], w3_send, w3_recv, plane_dev(*d)).start()

    for da in (2, 1, 3, 0):
        back(1, da)
        give_q(da)
        back(0, da)
        step1(da)
        step2(da)
    weight_term()
    for da in (2, 1, 3, 0):
        step2_sums(da)
    step3(2)
    send_a(2, 2, 2)
    weight_line()
    step3(1)
    send_a(1, 0, 1)
    step3(3)
    send_a(3, 1, -1)
    weight_plane()
    step3(0)
    for n in range(3):
        arrived(a_full.at[n], af_recv.at[n])
    part[0, 0:2] = part[0, 0:2] + (a_full[0] + a_full[1]) + a_full[2]

    total = part.at[0, pl.ds(0, 2)]

    @pl.when(native)
    def _():
        remote(total, xr.at[1], t_send.at[0], t_recv.at[1], twin).start()
        arrived(xr.at[0], t_recv.at[0])
        fgv[...] = (part[0, 0:2] + xr[0]).reshape(TILE, 256).T
        sent(total, t_send.at[0])

    @pl.when(jnp.logical_not(native))
    def _():
        remote(total, xr.at[0], t_send.at[0], t_recv.at[0], (at(y, z, 1 - xl, 1 - k), rep)).start()
        remote(total, xr.at[0], t_send.at[1], t_recv.at[0], (at(y, z, 1 - xl, 1 - k), 1 - rep)).start()
        arrived(xr.at[0], t_recv.at[0])
        arrived(xr.at[1], t_recv.at[1])
        fgv[...] = (xr[0] + xr[1]).reshape(TILE, 256).T
        sent(total, t_send.at[0])
        sent(total, t_send.at[1])

    fg_copy = pltpu.make_async_copy(fgv, fgrad_hbm, store_sem.at[1])
    fg_copy.start()

    arrived(wr3.at[pl.ds(0, 15)], w3_recv)
    for half_index in range(2):
        for i in range(8):
            for j in range(2):
                wgv[half_index * 64 + i * 8 : half_index * 64 + i * 8 + 8, j * TILE : j * TILE + TILE] = wr3[
                    i * 2 + j, half_index
                ]
    wg_copy = pltpu.make_async_copy(wgv, wgrad_hbm, store_sem.at[2])
    wg_copy.start()

    sent(feat.at[0, pl.ds(0, 4)], x_send)

    @pl.when(native)
    def _():
        sent(feat.at[0, pl.ds(0, 6)], n_send)

    sent(feat.at[0, pl.ds(0, 24)], f_send)
    sent(feat.at[0], fs_send)
    sent(swap.at[0], swap_send)
    sent(part.at[1], q_send)
    sent(b_opp, bo_send)
    sent(b_full, bf_send)
    sent(a_full, af_send)
    sent(wr1, w1_send)
    sent(wr2.at[pl.ds(0, 7)], w2_send)
    sent(wr3.at[pl.ds(0, 15)], w3_send)
    out_copy.wait()
    fg_copy.wait()
    wg_copy.wait()


def body(features, weight, tile_values, tile_pos, tile_counts, out_grad):
    dma = pltpu.SemaphoreType.DMA
    vm = pltpu.VMEM
    any_space = pl.BlockSpec(memory_space=pl.ANY)
    smem = pl.BlockSpec(memory_space=pltpu.SMEM)
    return pl.pallas_call(
        kernel,
        out_shape=(
            jax.ShapeDtypeStruct((256, 256), F32),
            jax.ShapeDtypeStruct((256, 128), F32),
            jax.ShapeDtypeStruct((128, 256), F32),
        ),
        in_specs=[any_space, any_space, any_space, smem, smem, any_space],
        out_specs=(any_space, any_space, any_space),
        scratch_shapes=[
            vm((16, 2, 3, TILE, TILE), F32),
            vm((256, 8192), BF16),
            vm((256, 8192), BF16),
            vm((2, 32, TILE, TILE), F32),
            vm((1024, 256), BF16),
            vm((256, 256), F32),
            vm((2, 256, TILE), F32),
            vm((TILE, 256), F32),
            vm((TILE, 256), F32),
            vm((256, 256), F32),
            vm((256, 256), F32),
            vm((256, 256), BF16),
            vm((256, 256), F32),
            vm((2, 32, 64, 256), F32),
            vm((32, 64, 256), F32),
            vm((4, 2, 64, 256), F32),
            vm((4, 2, 2, 64, 256), F32),
            vm((3, 2, 64, 256), F32),
            vm((2, 2, 64, 256), F32),
            vm((256, TILE), F32),
            vm((16, 8, TILE), F32),
            vm((15, 8, TILE), F32),
            vm((8, 8, TILE), F32),
            vm((16, 2, 8, TILE), F32),
            vm((TILE, 256), F32),
            dma, dma((2,)), dma, dma((3,)),
            dma, dma((32,)), dma, dma((16,)), dma, dma, dma, dma,
            dma, dma((16,)), dma, dma((4, 2)), dma, dma((4, 2, 2)), dma, dma((3,)),
            dma((2,)), dma((2,)), dma, dma, dma, dma, dma, dma,
        ],
        compiler_params=pltpu.CompilerParams(
            collective_id=0, has_side_effects=True, vmem_limit_bytes=60 * 1024 * 1024
        ),
        cost_estimate=pl.CostEstimate(flops=3_000_000_000, bytes_accessed=8_000_000, transcendentals=65536),
    )(
        features.reshape(2, TILE, TILE),
        weight,
        tile_values.reshape(16, 2, 2, 3, TILE, TILE),
        tile_pos.transpose(2, 0, 1),
        tile_counts,
        out_grad,
    )


def solution(mesh):
    return jax.shard_map(
        body,
        mesh=mesh,
        in_specs=(
            P("blk", None),
            P(),
            P("blk", None, None, None, None),
            P("blk", None, None),
            P("blk", None),
            P("blk", None),
        ),
        out_specs=(P("blk", None), P("blk", None), P()),
        check_vma=False,
    )
```

```python
import math

import jax
import jax.numpy as jnp
from jax import lax
from jax.experimental import pallas as pl
from jax.experimental.pallas import tpu as pltpu
from jax.sharding import PartitionSpec as P

HIGHEST = lax.Precision.HIGHEST
MESH = pl.DeviceIdType.MESH
F32, BF16 = jnp.float32, jnp.bfloat16
NODES = 16384
TILE = 128


def split(x):
    hi = x.astype(BF16)
    return hi, (x - hi.astype(F32)).astype(BF16)


def kernel(
    feat_hbm, weight_hbm, tiles_hbm, pos, counts, ograd_hbm,
    outv, fgv, wgv,
    tv, ah, al, feat, wside, acc, swap, agg_t, wt, og, pgrad, gs,
    part, sibq, b_opp, b_full, a_full, xr,
    wg, wr1, wr2, wr3,
    tile_sem, load_sem, first_sem,
    f_send, f_recv, fs_send, fs_recv, x_send, n_send, swap_send, swap_recv,
    q_send, q_recv, bo_send, bo_recv, bf_send, bf_recv, af_send, af_recv,
    t_send, t_recv, w1_send, w1_recv, w2_send, w2_recv, w3_send, w3_recv,
):
    blk, rep = lax.axis_index("blk"), lax.axis_index("rep")
    y, z = lax.rem(lax.div(blk, 16), 4), lax.rem(lax.div(blk, 4), 4)
    xl, k = lax.rem(lax.div(blk, 2), 2), lax.rem(blk, 2)
    native = k == rep

    def at(yy, zz, xx, kk):
        return ((lax.rem(yy + 8, 4) * 4 + lax.rem(zz + 8, 4)) * 2 + xx) * 2 + kk

    def near(da, db):
        return (at(y + da * (1 - k) + db * k, z + da * k + db * (1 - k), xl, k), rep)

    sibling = (at(y, z, xl, 1 - k), rep)

    def remote(src, dst, ssem, rsem, dev):
        return pltpu.make_async_remote_copy(
            src_ref=src, dst_ref=dst, send_sem=ssem, recv_sem=rsem, device_id=dev, device_id_type=MESH
        )

    def arrived(dst, rsem):
        remote(dst, dst, rsem, rsem, sibling).wait_recv()

    def sent(src, ssem):
        remote(src, src, ssem, ssem, sibling).wait_send()

    tile_copy = pltpu.make_async_copy(tiles_hbm.at[:, :, rep], tv, tile_sem)
    tile_copy.start()
    loads = [
        pltpu.make_async_copy(weight_hbm, wt, load_sem.at[0]),
        pltpu.make_async_copy(ograd_hbm, og, load_sem.at[1]),
    ]
    for c in loads:
        c.start()

    barrier = pltpu.get_barrier_semaphore()
    plane_peers = [(dy, dz) for dy in range(4) for dz in range(4) if (dy, dz) != (0, 0)]
    line_peers = [(i, j, l) for i in range(2) for j in range(2) for l in range(2) if (i, j, l) != (0, 0, 0)]

    def plane_dev(dy, dz):
        return (at(y + dy, z + dz, xl, k), rep)

    def line_dev(i, j, l):
        return (at(y, z, lax.rem(xl + j, 2), lax.rem(k + l, 2)), lax.rem(rep + i, 2))

    def over(m):
        return (at(y + m * k, z + m * (1 - k), 1 - xl, 1 - k), k)

    def over_from(m, i):
        return (at(y + m * (1 - k), z + m * k, 1 - xl, 1 - k), i)

    def greet(dev):
        pl.semaphore_signal(barrier, inc=1, device_id=dev, device_id_type=MESH)

    twin = (blk, 1 - rep)
    peers = [near(2, 0), near(0, 2), twin, near(1, 0), near(-1, 0), near(0, 1), near(0, -1), sibling]
    @pl.when(jnp.logical_not(native))
    def _():
        for m in (2, 1, -1):
            for i in range(2):
                greet(over_from(m, i))

    for i in range(2):
        greet((at(y, z, 1 - xl, 1 - k), i))
    for d in peers:
        greet(d)
    pl.semaphore_wait(barrier, len(peers) + 2 + 3)

    def spot(da, db, h):
        return (db % 4 * 4 + da % 4) * 2 + h

    def send_f(da, db, h, ma, mb):
        there = spot(da - ma, db - mb, h)
        remote(
            feat.at[0, spot(da, db, h)], feat.at[0, there], f_send, f_recv.at[there], near(ma, mb)
        ).start()

    def wait_f(da, db, h):
        i = spot(da, db, h)
        arrived(feat.at[0, i], f_recv.at[i])

    def give_f(da, db):
        i = spot(da, db, 0)
        remote(
            feat.at[0, pl.ds(i, 2)], feat.at[1, pl.ds(i, 2)], fs_send, fs_recv.at[i // 2], sibling
        ).start()

    def prep(kk, db):
        def one(da, carry):
            if kk == 0:
                own = k
            else:
                own = 1 - k
            yy = lax.rem(y + da * (1 - own) + db * own, 4)
            zz = lax.rem(z + da * own + db * (1 - own), 4)
            xx = lax.rem(xl + own + rep, 2)
            base = yy * 4 + zz
            c = (base * 2 + xx) * 2 + rep
            n = counts[0, c]
            p = [pos[s, 0, c] for s in range(3)]
            for q in range(4):
                s = jnp.where(p[0] == q, 0, jnp.where(p[1] == q, 1, 2))
                live = ((p[0] == q) & (n > 0)) | ((p[1] == q) & (n > 1)) | ((p[2] == q) & (n > 2))
                t = tv[base, xx, s] * jnp.where(live, 1.0, 0.0).astype(F32)
                hi, lo = split(t)
                col = pl.multiple_of((kk * 16 + db * 4 + da) * 256 + q % 2 * TILE, TILE)
                rows = slice(q // 2 * TILE, (q // 2 + 1) * TILE)
                ah[rows, pl.ds(col, TILE)] = hi
                al[rows, pl.ds(col, TILE)] = lo
            return carry

        lax.fori_loop(0, 4, one, 0)

    def multiply(kk, db):
        hi, lo = split(feat[kk, db * 8 : db * 8 + 8].reshape(1024, TILE))
        wside[:, 0:TILE] = hi
        wside[:, TILE : 2 * TILE] = lo
        cols = slice((kk * 16 + db * 4) * 256, (kk * 16 + db * 4 + 4) * 256)
        w = wside[...]
        acc[...] += jnp.dot(ah[:, cols], w, preferred_element_type=F32) + jnp.dot(
            al[:, cols], w, preferred_element_type=F32
        )

    half = lax.rem(k + rep, 2)
    for m in (0, 2, 1, -1):
        i = spot(-m, 0, 0) + half
        remote(feat_hbm.at[half], feat.at[0, i], x_send, f_recv.at[i], over(m)).start()
    first_copy = pltpu.make_async_copy(feat_hbm, feat.at[0, pl.ds(0, 2)], first_sem)

    @pl.when(native)
    def _():
        first_copy.start()
        for m in (2, 1, -1):
            for h in range(2):
                i = spot(-m, 0, h)
                remote(feat_hbm.at[h], feat.at[0, i], n_send, f_recv.at[i], near(m, 0)).start()
        first_copy.wait()

    @pl.when(jnp.logical_not(native))
    def _():
        for h in range(2):
            wait_f(0, 0, h)

    def spread(da):
        for h in range(2):
            send_f(da, 0, h, 0, 1)
            send_f(da, 0, 1 - h, 0, -1)
        give_f(da, 0)

    def pass_on(da):
        for h, db, m in ((0, 3, 1), (1, 1, -1)):
            wait_f(da, db, h)
            send_f(da, db, h, 0, m)
        for h, db in ((1, 3), (0, 1)):
            wait_f(da, db, h)
            give_f(da, db)

    def finish(da):
        for h in range(2):
            wait_f(da, 2, h)
        give_f(da, 2)

    def sib_multiply(db):
        for da in range(4):
            i = spot(da, db, 0)
            arrived(feat.at[1, pl.ds(i, 2)], fs_recv.at[i // 2])
        multiply(1, db)

    spread(0)
    acc[...] = jnp.zeros_like(acc)
    tile_copy.wait()
    prep(0, 0)
    for da in (2, 3, 1):
        for h in range(2):
            wait_f(da, 0, h)
        spread(da)
    prep(1, 0)
    prep(0, 3)
    pass_on(0)
    prep(0, 1)
    multiply(0, 0)
    pass_on(2)
    sib_multiply(0)
    pass_on(3)
    prep(1, 3)
    prep(1, 1)
    pass_on(1)
    multiply(0, 3)
    finish(0)
    multiply(0, 1)
    prep(0, 2)
    finish(2)
    sib_multiply(3)
    prep(1, 2)
    finish(3)
    sib_multiply(1)
    finish(1)
    multiply(0, 2)
    sib_multiply(2)

    swap[0] = acc[:, 0:TILE] + acc[:, TILE : 2 * TILE]
    c = remote(swap.at[0], swap.at[1], swap_send, swap_recv, twin)
    c.start()
    for l in loads:
        l.wait()
    c.wait_recv()
    agg = swap[0] + swap[1]
    w = wt[...]
    pre = jnp.dot(agg, w, precision=HIGHEST, preferred_element_type=F32)
    gate = jax.nn.sigmoid(pre)
    outv[...] = pre * gate
    pg = og[...] * gate * (1.0 + pre * (1.0 - gate))
    pgrad[...] = pg
    g_t = lax.dot_general(w, pg, (((1,), (1,)), ((), ())), precision=HIGHEST, preferred_element_type=F32)
    hi, lo = split(g_t)
    gs[0:TILE] = hi
    gs[TILE : 2 * TILE] = lo

    def back(kk, db):
        cols = slice((kk * 16 + db * 4) * 256, (kk * 16 + db * 4 + 4) * 256)
        main = jnp.dot(gs[...], ah[:, cols], preferred_element_type=F32)
        rest = jnp.dot(gs[0:TILE], al[:, cols], preferred_element_type=F32)
        total = main[0:TILE] + main[TILE : 2 * TILE] + rest
        for da in range(4):
            for h in range(2):
                part[kk, spot(da, db, h)] = total[h * 64 : h * 64 + 64, da * 256 : da * 256 + 256]

    def give_q(db):
        for da in (2, 1, 3, 0):
            i = spot(da, db, 0)
            remote(
                part.at[1, pl.ds(i, 2)], sibq.at[pl.ds(i, 2)], q_send, q_recv.at[i // 2], sibling
            ).start()

    def take_q(da, db):
        i = spot(da, db, 0)
        arrived(sibq.at[pl.ds(i, 2)], q_recv.at[i // 2])
        part[0, i : i + 2] = part[0, i : i + 2] + sibq[i : i + 2]

    def step1(da):
        take_q(da, 2)
        for h, m in ((0, 1), (1, -1)):
            remote(
                part.at[0, spot(da, 2, h)], b_opp.at[da, h], bo_send, bo_recv.at[da, h], near(0, m)
            ).start()

    def send_full(da, db, h, n, m):
        remote(
            part.at[0, spot(da, db, h)], b_full.at[da, n, h], bf_send, bf_recv.at[da, n, h], near(0, m)
        ).start()

    def step2(da, db):
        take_q(da, db)
        if db == 1:
            send_full(da, 1, 1, 0, 1)
        else:
            send_full(da, 3, 0, 1, -1)

    def step2_sums(da):
        for db, h, m in ((1, 0, 1), (3, 1, -1)):
            arrived(b_opp.at[da, h], bo_recv.at[da, h])
            i = spot(da, db, h)
            part[0, i] = part[0, i] + b_opp[da, h]
            send_full(da, db, h, h, m)

    def step3(da):
        take_q(da, 0)
        for n in range(2):
            for h in range(2):
                arrived(b_full.at[da, n, h], bf_recv.at[da, n, h])
        i = spot(da, 0, 0)
        part[0, i : i + 2] = part[0, i : i + 2] + (b_full[da, 0] + b_full[da, 1])

    def send_a(da, n, m):
        i = spot(da, 0, 0)
        remote(part.at[0, pl.ds(i, 2)], a_full.at[n], af_send, af_recv.at[n], near(m, 0)).start()

    def weight_term():
        agg_t[...] = (swap[0] + swap[1]).T
        rows = agg_t[pl.ds(pl.multiple_of(rep * 64, 64), 64), :]
        term = jnp.dot(rows, pgrad[...], precision=HIGHEST, preferred_element_type=F32)
        for i in range(8):
            for j in range(2):
                wg[i * 2 + j] = term[i * 8 : i * 8 + 8, j * TILE : j * TILE + TILE]
        for dy, dz in plane_peers:
            there = lax.rem(y + dy, 4) * 4 + lax.rem(z + dz, 4)
            remote(wg.at[there], wr1.at[dy * 4 + dz - 1], w1_send, w1_recv, plane_dev(dy, dz)).start()

    here = y * 4 + z
    line = (rep * 2 + xl) * 2 + k

    def weight_line():
        arrived(wr1, w1_recv)
        total = wg[here]
        for i in range(15):
            total = total + wr1[i]
        wr2[line] = total
        for d in line_peers:
            remote(wr2.at[line], wr2.at[line], w2_send, w2_recv, line_dev(*d)).start()

    def weight_plane():
        arrived(wr2.at[pl.ds(0, 7)], w2_recv)
        for i in range(2):
            total = (wr2[4 * i] + wr2[4 * i + 1]) + (wr2[4 * i + 2] + wr2[4 * i + 3])
            wr3[here, i] = total * (1.0 / math.sqrt(NODES))
        for d in plane_peers:
            remote(wr3.at[here], wr3.at[here], w3_send, w3_recv, plane_dev(*d)).start()

    for db in (2, 1, 3, 0):
        back(1, db)
        give_q(db)
        back(0, db)
        for da in (2, 1, 3, 0):
            if db == 2:
                step1(da)
            elif db != 0:
                step2(da, db)
        if db == 3:
            weight_term()
    for da in (2, 1, 3, 0):
        step2_sums(da)
    step3(2)
    send_a(2, 2, 2)
    weight_line()
    step3(1)
    send_a(1, 0, 1)
    step3(3)
    send_a(3, 1, -1)
    weight_plane()
    step3(0)
    for n in range(3):
        arrived(a_full.at[n], af_recv.at[n])
    part[0, 0:2] = part[0, 0:2] + (a_full[0] + a_full[1]) + a_full[2]

    total = part.at[0, pl.ds(0, 2)]

    @pl.when(native)
    def _():
        remote(total, xr.at[1], t_send.at[0], t_recv.at[1], twin).start()
        arrived(xr.at[0], t_recv.at[0])
        fgv[...] = (part[0, 0:2] + xr[0]).reshape(TILE, 256).T
        sent(total, t_send.at[0])

    @pl.when(jnp.logical_not(native))
    def _():
        remote(total, xr.at[0], t_send.at[0], t_recv.at[0], (at(y, z, 1 - xl, 1 - k), rep)).start()
        remote(total, xr.at[0], t_send.at[1], t_recv.at[0], (at(y, z, 1 - xl, 1 - k), 1 - rep)).start()
        arrived(xr.at[0], t_recv.at[0])
        arrived(xr.at[1], t_recv.at[1])
        fgv[...] = (xr[0] + xr[1]).reshape(TILE, 256).T
        sent(total, t_send.at[0])
        sent(total, t_send.at[1])


    arrived(wr3.at[pl.ds(0, 15)], w3_recv)
    for half_index in range(2):
        for i in range(8):
            for j in range(2):
                wgv[half_index * 64 + i * 8 : half_index * 64 + i * 8 + 8, j * TILE : j * TILE + TILE] = wr3[
                    i * 2 + j, half_index
                ]

    sent(feat.at[0, pl.ds(0, 4)], x_send)

    @pl.when(native)
    def _():
        sent(feat.at[0, pl.ds(0, 6)], n_send)

    sent(feat.at[0, pl.ds(0, 24)], f_send)
    sent(feat.at[0], fs_send)
    sent(swap.at[0], swap_send)
    sent(part.at[1], q_send)
    sent(b_opp, bo_send)
    sent(b_full, bf_send)
    sent(a_full, af_send)
    sent(wr1, w1_send)
    sent(wr2.at[pl.ds(0, 7)], w2_send)
    sent(wr3.at[pl.ds(0, 15)], w3_send)


def body(features, weight, tile_values, tile_pos, tile_counts, out_grad):
    dma = pltpu.SemaphoreType.DMA
    vm = pltpu.VMEM
    any_space = pl.BlockSpec(memory_space=pl.ANY)
    smem = pl.BlockSpec(memory_space=pltpu.SMEM)
    vspace = pl.BlockSpec(memory_space=pltpu.VMEM)
    shapes = (
        jax.ShapeDtypeStruct((256, 256), F32),
        jax.ShapeDtypeStruct((256, 128), F32),
        jax.ShapeDtypeStruct((128, 256), F32),
    )
    return pl.pallas_call(
        kernel,
        out_shape=tuple(pltpu.VMEM(x.shape, x.dtype) for x in shapes),
        in_specs=[any_space, any_space, any_space, smem, smem, any_space],
        out_specs=(vspace,) * 3,
        scratch_shapes=[
            vm((16, 2, 3, TILE, TILE), F32),
            vm((256, 8192), BF16),
            vm((256, 8192), BF16),
            vm((2, 32, TILE, TILE), F32),
            vm((1024, 256), BF16),
            vm((256, 256), F32),
            vm((2, 256, TILE), F32),
            vm((TILE, 256), F32),
            vm((TILE, 256), F32),
            vm((256, 256), F32),
            vm((256, 256), F32),
            vm((256, 256), BF16),
            vm((2, 32, 64, 256), F32),
            vm((32, 64, 256), F32),
            vm((4, 2, 64, 256), F32),
            vm((4, 2, 2, 64, 256), F32),
            vm((3, 2, 64, 256), F32),
            vm((2, 2, 64, 256), F32),
            vm((16, 8, TILE), F32),
            vm((15, 8, TILE), F32),
            vm((8, 8, TILE), F32),
            vm((16, 2, 8, TILE), F32),
            dma, dma((2,)), dma,
            dma, dma((32,)), dma, dma((16,)), dma, dma, dma, dma,
            dma, dma((16,)), dma, dma((4, 2)), dma, dma((4, 2, 2)), dma, dma((3,)),
            dma((2,)), dma((2,)), dma, dma, dma, dma, dma, dma,
        ],
        compiler_params=pltpu.CompilerParams(
            collective_id=0, has_side_effects=True, vmem_limit_bytes=60 * 1024 * 1024
        ),
        cost_estimate=pl.CostEstimate(flops=3_000_000_000, bytes_accessed=8_000_000, transcendentals=65536),
    )(
        features.reshape(2, TILE, TILE),
        weight,
        tile_values.reshape(16, 2, 2, 3, TILE, TILE),
        tile_pos.transpose(2, 0, 1),
        tile_counts,
        out_grad,
    )


def solution(mesh):
    return jax.shard_map(
        body,
        mesh=mesh,
        in_specs=(
            P("blk", None),
            P(),
            P("blk", None, None, None, None),
            P("blk", None, None),
            P("blk", None),
            P("blk", None),
        ),
        out_specs=(P("blk", None), P("blk", None), P()),
        check_vma=False,
    )
```

```python
import math

import jax
import jax.numpy as jnp
from jax import lax
from jax.experimental import pallas as pl
from jax.experimental.pallas import tpu as pltpu
from jax.sharding import PartitionSpec as P

HIGHEST = lax.Precision.HIGHEST
MESH = pl.DeviceIdType.MESH
F32, BF16 = jnp.float32, jnp.bfloat16
NODES = 16384
TILE = 128


def split(x):
    hi = x.astype(BF16)
    return hi, (x - hi.astype(F32)).astype(BF16)


def kernel(
    feat_hbm, weight_hbm, tiles_hbm, pos_hbm, counts_hbm, ograd_hbm,
    outv, fgv, wgv,
    pos, counts, tv, ah, al, feat, wside, acc, swap, agg_t, wt, og, pgrad, gs,
    part, sibq, b_opp, b_full, a_full, xr,
    wg, wr1, wr2, wr3,
    tile_sem, load_sem, first_sem,
    f_send, f_recv, f2_recv, fs_send, fs_recv, x_send, n_send, swap_send, swap_recv,
    q_send, q_recv, bo_send, bo_recv, bf_send, bf_recv, af_send, af_recv,
    t_send, t_recv, w1_send, w1_recv, w2_send, w2_recv, w3_send, w3_recv,
):
    blk, rep = lax.axis_index("blk"), lax.axis_index("rep")
    y, z = lax.rem(lax.div(blk, 16), 4), lax.rem(lax.div(blk, 4), 4)
    xl, k = lax.rem(lax.div(blk, 2), 2), lax.rem(blk, 2)
    native = k == rep

    def at(yy, zz, xx, kk):
        return ((lax.rem(yy + 8, 4) * 4 + lax.rem(zz + 8, 4)) * 2 + xx) * 2 + kk

    def near(da, db):
        return (at(y + da * (1 - k) + db * k, z + da * k + db * (1 - k), xl, k), rep)

    sibling = (at(y, z, xl, 1 - k), rep)

    def remote(src, dst, ssem, rsem, dev):
        return pltpu.make_async_remote_copy(
            src_ref=src, dst_ref=dst, send_sem=ssem, recv_sem=rsem, device_id=dev, device_id_type=MESH
        )

    def arrived(dst, rsem):
        remote(dst, dst, rsem, rsem, sibling).wait_recv()

    def sent(src, ssem):
        remote(src, src, ssem, ssem, sibling).wait_send()

    tile_copy = pltpu.make_async_copy(tiles_hbm.at[:, :, rep], tv, tile_sem)
    tile_copy.start()
    loads = [
        pltpu.make_async_copy(weight_hbm, wt, load_sem.at[0]),
        pltpu.make_async_copy(ograd_hbm, og, load_sem.at[1]),
    ]
    places = [
        pltpu.make_async_copy(pos_hbm, pos, load_sem.at[2]),
        pltpu.make_async_copy(counts_hbm, counts, load_sem.at[3]),
    ]
    for c in places + loads:
        c.start()

    barrier = pltpu.get_barrier_semaphore()
    plane_peers = [(dy, dz) for dy in range(4) for dz in range(4) if (dy, dz) != (0, 0)]
    line_peers = [(i, j, l) for i in range(2) for j in range(2) for l in range(2) if (i, j, l) != (0, 0, 0)]

    def plane_dev(dy, dz):
        return (at(y + dy, z + dz, xl, k), rep)

    def line_dev(i, j, l):
        return (at(y, z, lax.rem(xl + j, 2), lax.rem(k + l, 2)), lax.rem(rep + i, 2))

    def near_in(u, mf, mg):
        return near(mf, mg) if u == 0 else near(mg, mf)

    half = lax.rem(k + rep, 2)
    along_y = k * (1 - half) + (1 - k) * half

    def over(m):
        return (at(y + m * along_y, z + m * (1 - along_y), 1 - xl, 1 - k), k)

    def over_from(m, i):
        u = lax.rem(1 - k + i, 2)
        c = (1 - k) * (1 - u) + k * u
        return (at(y + m * c, z + m * (1 - c), 1 - xl, 1 - k), i)

    def greet(dev):
        pl.semaphore_signal(barrier, inc=1, device_id=dev, device_id_type=MESH)

    twin = (blk, 1 - rep)
    peers = [near(2, 0), near(0, 2), twin, near(1, 0), near(-1, 0), near(0, 1), near(0, -1), sibling]
    @pl.when(jnp.logical_not(native))
    def _():
        for m in (2, 1, -1):
            for i in range(2):
                greet(over_from(m, i))

    for i in range(2):
        greet((at(y, z, 1 - xl, 1 - k), i))
    for d in peers:
        greet(d)
    pl.semaphore_wait(barrier, len(peers) + 2 + 3)

    def unit(u, f, g):
        return g % 4 * 8 + u * 4 + f % 4

    def wait_f(u, f, g):
        i = unit(u, f, g)
        arrived(feat.at[0, i], f_recv.at[i])

    def give_f(u, f, g):
        i = unit(u, f, g)
        remote(feat.at[0, i], feat.at[1, i], fs_send, fs_recv.at[i], sibling).start()

    def quarter(ref, q):
        return ref.at[pl.ds(q * 64, 64)]

    def prep(kk, g):
        own = k if kk == 0 else 1 - k
        xx = lax.rem(xl + own + rep, 2)

        def one(f, carry):
            for u in range(2):
                da, db = (f, g) if u == 0 else (g, f)
                yy = lax.rem(y + da * (1 - own) + db * own, 4)
                zz = lax.rem(z + da * own + db * (1 - own), 4)
                base = yy * 4 + zz
                c = (base * 2 + xx) * 2 + rep
                n = counts[0, c]
                p = [pos[s, 0, c] for s in range(3)]
                col = pl.multiple_of((kk * 32 + g * 8 + u * 4 + f) * TILE, TILE)
                for t in range(2):
                    q = t * 2 + u
                    s = jnp.where(p[0] == q, 0, jnp.where(p[1] == q, 1, 2))
                    live = ((p[0] == q) & (n > 0)) | ((p[1] == q) & (n > 1)) | ((p[2] == q) & (n > 2))
                    hi, lo = split(tv[base, xx, s] * jnp.where(live, 1.0, 0.0).astype(F32))
                    ah[t * TILE : (t + 1) * TILE, pl.ds(col, TILE)] = hi
                    al[t * TILE : (t + 1) * TILE, pl.ds(col, TILE)] = lo
            return carry

        lax.fori_loop(0, 4, one, 0)

    def multiply(kk, db, last=False):
        hi, lo = split(feat[kk, db * 8 : db * 8 + 8].reshape(1024, TILE))
        wside[:, 0:TILE] = hi
        wside[:, TILE : 2 * TILE] = lo
        cols = slice((kk * 16 + db * 4) * 256, (kk * 16 + db * 4 + 4) * 256)
        w = wside[...]
        for rows in (slice(0, TILE), slice(TILE, 2 * TILE)):
            new = acc[rows] + (
                jnp.dot(ah[rows, cols], w, preferred_element_type=F32)
                + jnp.dot(al[rows, cols], w, preferred_element_type=F32)
            )
            if last:
                swap[0, rows] = new[:, 0:TILE] + new[:, TILE : 2 * TILE]
                t = rows.start // TILE
                remote(swap.at[0, pl.ds(t * TILE, TILE)], swap.at[1, pl.ds(t * TILE, TILE)], swap_send,
                       swap_recv.at[t], twin).start()
            else:
                acc[rows] = new

    for m in (0, 2, 1, -1):
        i = half * 4 + (-m % 4)
        remote(feat_hbm.at[half], feat.at[0, i], x_send, f_recv.at[i], over(m)).start()
    first_copies = [pltpu.make_async_copy(feat_hbm.at[u], feat.at[0, u * 4], first_sem.at[u]) for u in range(2)]

    @pl.when(native)
    def _():
        for c in first_copies:
            c.start()
        for m in (2, 1, -1):
            for u in range(2):
                i = unit(u, -m, 0)
                remote(feat_hbm.at[u], feat.at[0, i], n_send, f_recv.at[i], near_in(u, m, 0)).start()
        for c in first_copies:
            c.wait()

    @pl.when(jnp.logical_not(native))
    def _():
        for u in range(2):
            wait_f(u, 0, 0)

    def spread(f):
        for u in range(2):
            if f != 0:
                wait_f(u, f, 0)
            for m in (1, -1):
                i = unit(u, f, -m)
                remote(feat.at[0, unit(u, f, 0)], feat.at[0, i], f_send, f_recv.at[i], near_in(u, 0, m)).start()
            give_f(u, f, 0)

    def pass_on(f):
        for u in range(2):
            i = unit(u, f, 2)
            for q, g, m, sem in ((0, 3, 1, f_recv.at[i]), (1, 1, -1, f2_recv.at[u * 4 + f])):
                wait_f(u, f, g)
                remote(
                    quarter(feat.at[0, unit(u, f, g)], q), quarter(feat.at[0, i], q), f_send, sem, near_in(u, 0, m)
                ).start()
                give_f(u, f, g)

    def finish(f):
        for u in range(2):
            i = unit(u, f, 2)
            arrived(quarter(feat.at[0, i], 0), f_recv.at[i])
            arrived(quarter(feat.at[0, i], 1), f2_recv.at[u * 4 + f])
            give_f(u, f, 2)

    def sib_multiply(g):
        for i in range(g * 8, g * 8 + 8):
            arrived(feat.at[1, i], fs_recv.at[i])
        multiply(1, g, g == 2)

    spread(0)
    acc[...] = jnp.zeros_like(acc)
    tile_copy.wait()
    for c in places:
        c.wait()
    prep(0, 0)
    for f in (2, 3, 1):
        spread(f)
    prep(1, 0)
    prep(0, 3)
    pass_on(0)
    prep(0, 1)
    multiply(0, 0)
    pass_on(2)
    sib_multiply(0)
    pass_on(3)
    prep(1, 3)
    prep(1, 1)
    pass_on(1)
    multiply(0, 3)
    finish(0)
    multiply(0, 1)
    prep(0, 2)
    finish(2)
    sib_multiply(3)
    prep(1, 2)
    finish(3)
    sib_multiply(1)
    finish(1)
    multiply(0, 2)
    sib_multiply(2)

    for l in loads:
        l.wait()
    w = wt[...]
    for t in range(2):
        rows = slice(t * TILE, t * TILE + TILE)
        arrived(swap.at[1, pl.ds(t * TILE, TILE)], swap_recv.at[t])
        agg = swap[0, rows] + swap[1, rows]
        pre = jnp.dot(agg, w, precision=HIGHEST, preferred_element_type=F32)
        gate = jax.nn.sigmoid(pre)
        outv[rows] = pre * gate
        pg = og[rows] * gate * (1.0 + pre * (1.0 - gate))
        pgrad[rows] = pg
        g_t = lax.dot_general(w, pg, (((1,), (1,)), ((), ())), precision=HIGHEST, preferred_element_type=F32)
        hi, lo = split(g_t)
        gs[0:TILE, rows] = hi
        gs[TILE : 2 * TILE, rows] = lo

    def back(kk, g):
        cols = slice((kk * 4 + g) * 1024, (kk * 4 + g + 1) * 1024)
        main = jnp.dot(gs[...], ah[:, cols], preferred_element_type=F32)
        rest = jnp.dot(gs[0:TILE], al[:, cols], preferred_element_type=F32)
        total = main[0:TILE] + main[TILE : 2 * TILE] + rest
        for i in range(8):
            part[kk, g * 8 + i] = total[:, i * TILE : i * TILE + TILE]

    def give_q(g):
        for f in (2, 1, 3, 0):
            for u in range(2):
                i = unit(u, f, g)
                remote(part.at[1, i], sibq.at[i], q_send, q_recv.at[i], sibling).start()

    def take_q(i):
        arrived(sibq.at[i], q_recv.at[i])
        part[0, i] = part[0, i] + sibq[i]

    def step1(u, f):
        i, j = unit(u, f, 2), u * 4 + f
        take_q(i)
        for q, m in ((0, 1), (1, -1)):
            remote(
                quarter(part.at[0, i], q), b_opp.at[q, j], bo_send, bo_recv.at[q, j], near_in(u, 0, m)
            ).start()

    def send_full(u, f, g, q):
        n, j = g // 2, u * 4 + f
        remote(
            quarter(part.at[0, unit(u, f, g)], q), quarter(b_full.at[n, j], q), bf_send, bf_recv.at[n, j, q],
            near_in(u, 0, 1 - 2 * n),
        ).start()

    def step2(u, f, g):
        take_q(unit(u, f, g))
        send_full(u, f, g, 1 - g // 2)

    def step2_sums(u, f):
        for q in range(2):
            g, j = 1 + 2 * q, u * 4 + f
            i, rows = unit(u, f, g), slice(q * 64, q * 64 + 64)
            arrived(b_opp.at[q, j], bo_recv.at[q, j])
            part[0, i, rows] = part[0, i, rows] + b_opp[q, j]
            send_full(u, f, g, q)

    def step3(u, f):
        i, j = unit(u, f, 0), u * 4 + f
        take_q(i)
        for n in range(2):
            for q in range(2):
                arrived(quarter(b_full.at[n, j], q), bf_recv.at[n, j, q])
        part[0, i] = part[0, i] + (b_full[0, j] + b_full[1, j])

    def send_a(u, f, n, m):
        remote(part.at[0, unit(u, f, 0)], a_full.at[n, u], af_send, af_recv.at[n, u], near_in(u, m, 0)).start()

    def weight_term():
        agg_t[...] = (swap[0] + swap[1]).T
        rows = agg_t[pl.ds(pl.multiple_of(rep * 64, 64), 64), :]
        term = jnp.dot(rows, pgrad[...], precision=HIGHEST, preferred_element_type=F32)
        for i in range(8):
            for j in range(2):
                wg[i * 2 + j] = term[i * 8 : i * 8 + 8, j * TILE : j * TILE + TILE]
        for dy, dz in plane_peers:
            there = lax.rem(y + dy, 4) * 4 + lax.rem(z + dz, 4)
            remote(wg.at[there], wr1.at[dy * 4 + dz - 1], w1_send, w1_recv, plane_dev(dy, dz)).start()

    here = y * 4 + z
    line = (rep * 2 + xl) * 2 + k

    def weight_line():
        arrived(wr1, w1_recv)
        total = wg[here]
        for i in range(15):
            total = total + wr1[i]
        wr2[line] = total
        for d in line_peers:
            remote(wr2.at[line], wr2.at[line], w2_send, w2_recv, line_dev(*d)).start()

    def weight_plane():
        arrived(wr2.at[pl.ds(0, 7)], w2_recv)
        for i in range(2):
            total = (wr2[4 * i] + wr2[4 * i + 1]) + (wr2[4 * i + 2] + wr2[4 * i + 3])
            wr3[here, i] = total * (1.0 / math.sqrt(NODES))
        for d in plane_peers:
            remote(wr3.at[here], wr3.at[here], w3_send, w3_recv, plane_dev(*d)).start()

    both = [(u, f) for f in (2, 1, 3, 0) for u in range(2)]
    for g in (2, 1, 3, 0):
        back(1, g)
        give_q(g)
        back(0, g)
        for u, f in both:
            if g == 2:
                step1(u, f)
            elif g != 0:
                step2(u, f, g)
        if g == 3:
            weight_term()
    for u, f in both:
        step2_sums(u, f)
    for f, n, m in ((2, 2, 2), (1, 0, 1), (3, 1, -1)):
        for u in range(2):
            step3(u, f)
            send_a(u, f, n, m)
        if f == 2:
            weight_line()
    weight_plane()
    for u in range(2):
        step3(u, 0)

    other = at(y, z, 1 - xl, 1 - k)
    for u in range(2):
        for n in range(3):
            arrived(a_full.at[n, u], af_recv.at[n, u])
        i = unit(u, 0, 0)
        part[0, i] = part[0, i] + (a_full[0, u] + a_full[1, u]) + a_full[2, u]
        total = part.at[0, i]

        @pl.when(native)
        def _():
            remote(total, xr.at[1, u], t_send.at[0], t_recv.at[1, u], twin).start()

        @pl.when(jnp.logical_not(native))
        def _():
            remote(total, xr.at[0, u], t_send.at[0], t_recv.at[0, u], (other, rep)).start()
            remote(total, xr.at[0, u], t_send.at[1], t_recv.at[0, u], (other, 1 - rep)).start()

    for u in range(2):
        arrived(xr.at[0, u], t_recv.at[0, u])

    @pl.when(native)
    def _():
        for u in range(2):
            fgv[u * TILE : (u + 1) * TILE] = (part[0, unit(u, 0, 0)] + xr[0, u]).T
        sent(xr.at[0], t_send.at[0])

    @pl.when(jnp.logical_not(native))
    def _():
        for u in range(2):
            arrived(xr.at[1, u], t_recv.at[1, u])
            fgv[u * TILE : (u + 1) * TILE] = (xr[1, u] + xr[0, u]).T
        sent(xr.at[0], t_send.at[0])
        sent(xr.at[0], t_send.at[1])

    arrived(wr3.at[pl.ds(0, 15)], w3_recv)
    for half_index in range(2):
        for i in range(8):
            for j in range(2):
                wgv[half_index * 64 + i * 8 : half_index * 64 + i * 8 + 8, j * TILE : j * TILE + TILE] = wr3[
                    i * 2 + j, half_index
                ]

    sent(feat.at[0, pl.ds(0, 4)], x_send)

    @pl.when(native)
    def _():
        sent(feat.at[0, pl.ds(0, 6)], n_send)

    sent(feat.at[0, pl.ds(0, 24)], f_send)
    sent(feat.at[0], fs_send)
    sent(swap.at[0], swap_send)
    sent(part.at[1], q_send)
    sent(b_opp, bo_send)
    sent(b_full, bf_send)
    sent(a_full, af_send)
    sent(wr1, w1_send)
    sent(wr2.at[pl.ds(0, 7)], w2_send)
    sent(wr3.at[pl.ds(0, 15)], w3_send)


def body(features, weight, tile_values, tile_pos, tile_counts, out_grad):
    dma = pltpu.SemaphoreType.DMA
    vm = pltpu.VMEM
    any_space = pl.BlockSpec(memory_space=pl.ANY)
    vspace = pl.BlockSpec(memory_space=pltpu.VMEM)
    shapes = (
        jax.ShapeDtypeStruct((256, 256), F32),
        jax.ShapeDtypeStruct((256, 128), F32),
        jax.ShapeDtypeStruct((128, 256), F32),
    )
    return pl.pallas_call(
        kernel,
        out_shape=tuple(pltpu.VMEM(x.shape, x.dtype) for x in shapes),
        in_specs=[any_space] * 6,
        out_specs=(vspace,) * 3,
        scratch_shapes=[
            pltpu.SMEM((3, 1, 64), jnp.int32),
            pltpu.SMEM((1, 64), jnp.int32),
            vm((16, 2, 3, TILE, TILE), F32),
            vm((256, 8192), BF16),
            vm((256, 8192), BF16),
            vm((2, 32, TILE, TILE), F32),
            vm((1024, 256), BF16),
            vm((256, 256), F32),
            vm((2, 256, TILE), F32),
            vm((TILE, 256), F32),
            vm((TILE, 256), F32),
            vm((256, 256), F32),
            vm((256, 256), F32),
            vm((256, 256), BF16),
            vm((2, 32, TILE, TILE), F32),
            vm((32, TILE, TILE), F32),
            vm((2, 8, 64, TILE), F32),
            vm((2, 8, TILE, TILE), F32),
            vm((3, 2, TILE, TILE), F32),
            vm((2, 2, TILE, TILE), F32),
            vm((16, 8, TILE), F32),
            vm((15, 8, TILE), F32),
            vm((8, 8, TILE), F32),
            vm((16, 2, 8, TILE), F32),
            dma, dma((4,)), dma((2,)),
            dma, dma((32,)), dma((8,)), dma, dma((32,)), dma, dma, dma, dma((2,)),
            dma, dma((32,)), dma, dma((2, 8)), dma, dma((2, 8, 2)), dma, dma((3, 2)),
            dma((2,)), dma((2, 2)), dma, dma, dma, dma, dma, dma,
        ],
        compiler_params=pltpu.CompilerParams(
            collective_id=0, has_side_effects=True, vmem_limit_bytes=60 * 1024 * 1024
        ),
        cost_estimate=pl.CostEstimate(flops=3_000_000_000, bytes_accessed=8_000_000, transcendentals=65536),
    )(
        features.reshape(2, TILE, TILE),
        weight,
        tile_values.reshape(16, 2, 2, 3, TILE, TILE),
        tile_pos.transpose(2, 0, 1),
        tile_counts,
        out_grad,
    )


def solution(mesh):
    return jax.shard_map(
        body,
        mesh=mesh,
        in_specs=(
            P("blk", None),
            P(),
            P("blk", None, None, None, None),
            P("blk", None, None),
            P("blk", None),
            P("blk", None),
        ),
        out_specs=(P("blk", None), P("blk", None), P()),
        check_vma=False,
    )
```

```python
import math

import jax
import jax.numpy as jnp
from jax import lax
from jax.experimental import pallas as pl
from jax.experimental.pallas import tpu as pltpu
from jax.sharding import PartitionSpec as P

HIGHEST = lax.Precision.HIGHEST
MESH = pl.DeviceIdType.MESH
F32, BF16 = jnp.float32, jnp.bfloat16
NODES = 16384
TILE = 128


def split(x):
    hi = x.astype(BF16)
    return hi, (x - hi.astype(F32)).astype(BF16)


def kernel(
    feat_hbm, weight_hbm, tiles_hbm, pos_hbm, counts_hbm, ograd_hbm,
    outv, fgv, wgv,
    pos, counts, tv, ah, al, feat, wside, acc, swap, agg_t, wt, og, pgrad, gs,
    part, sibq, b_opp, b_full, a_full, xr,
    wg, wr1, wr2, wr3,
    tile_sem, load_sem, first_sem,
    f_send, f_recv, f2_recv, fs_send, fs_recv, x_send, n_send, swap_send, swap_recv,
    q_send, q_recv, bo_send, bo_recv, bf_send, bf_recv, af_send, af_recv,
    t_send, t_recv, w1_send, w1_recv, w2_send, w2_recv, w3_send, w3_recv,
):
    blk, rep = lax.axis_index("blk"), lax.axis_index("rep")
    y, z = lax.rem(lax.div(blk, 16), 4), lax.rem(lax.div(blk, 4), 4)
    xl, k = lax.rem(lax.div(blk, 2), 2), lax.rem(blk, 2)
    native = k == rep

    def at(yy, zz, xx, kk):
        return ((lax.rem(yy + 8, 4) * 4 + lax.rem(zz + 8, 4)) * 2 + xx) * 2 + kk

    def near(da, db):
        return (at(y + da * (1 - k) + db * k, z + da * k + db * (1 - k), xl, k), rep)

    sibling = (at(y, z, xl, 1 - k), rep)

    def remote(src, dst, ssem, rsem, dev):
        return pltpu.make_async_remote_copy(
            src_ref=src, dst_ref=dst, send_sem=ssem, recv_sem=rsem, device_id=dev, device_id_type=MESH
        )

    def arrived(dst, rsem):
        remote(dst, dst, rsem, rsem, sibling).wait_recv()

    def sent(src, ssem):
        remote(src, src, ssem, ssem, sibling).wait_send()

    tile_copy = pltpu.make_async_copy(tiles_hbm.at[:, :, rep], tv, tile_sem)
    tile_copy.start()
    loads = [
        pltpu.make_async_copy(weight_hbm, wt, load_sem.at[0]),
        pltpu.make_async_copy(ograd_hbm, og, load_sem.at[1]),
    ]
    places = [
        pltpu.make_async_copy(pos_hbm, pos, load_sem.at[2]),
        pltpu.make_async_copy(counts_hbm, counts, load_sem.at[3]),
    ]
    for c in places + loads:
        c.start()

    barrier = pltpu.get_barrier_semaphore()
    plane_peers = [(dy, dz) for dy in range(4) for dz in range(4) if (dy, dz) != (0, 0)]
    line_peers = [(i, j, l) for i in range(2) for j in range(2) for l in range(2) if (i, j, l) != (0, 0, 0)]

    def plane_dev(dy, dz):
        return (at(y + dy, z + dz, xl, k), rep)

    def line_dev(i, j, l):
        return (at(y, z, lax.rem(xl + j, 2), lax.rem(k + l, 2)), lax.rem(rep + i, 2))

    def near_in(u, mf, mg):
        return near(mf, mg) if u == 0 else near(mg, mf)

    half = lax.rem(k + rep, 2)
    along_y = k * (1 - half) + (1 - k) * half

    def over(m):
        return (at(y + m * along_y, z + m * (1 - along_y), 1 - xl, 1 - k), k)

    def over_from(m, i):
        u = lax.rem(1 - k + i, 2)
        c = (1 - k) * (1 - u) + k * u
        return (at(y + m * c, z + m * (1 - c), 1 - xl, 1 - k), i)

    def greet(dev):
        pl.semaphore_signal(barrier, inc=1, device_id=dev, device_id_type=MESH)

    twin = (blk, 1 - rep)
    peers = [near(2, 0), near(0, 2), twin, near(1, 0), near(-1, 0), near(0, 1), near(0, -1), sibling]
    @pl.when(jnp.logical_not(native))
    def _():
        for m in (2, 1, -1):
            for i in range(2):
                greet(over_from(m, i))

    for i in range(2):
        greet((at(y, z, 1 - xl, 1 - k), i))
    for d in peers:
        greet(d)
    pl.semaphore_wait(barrier, len(peers) + 2 + 3)

    def unit(u, f, g):
        return g % 4 * 8 + u * 4 + f % 4

    def wait_f(u, f, g):
        i = unit(u, f, g)
        arrived(feat.at[0, i], f_recv.at[i])

    def give_f(u, f, g):
        i = unit(u, f, g)
        remote(feat.at[0, i], feat.at[1, i], fs_send, fs_recv.at[i], sibling).start()

    def quarter(ref, q):
        return ref.at[pl.ds(q * 64, 64)]

    def prep(kk, g):
        own = k if kk == 0 else 1 - k
        xx = lax.rem(xl + own + rep, 2)

        def one(f, carry):
            for u in range(2):
                da, db = (f, g) if u == 0 else (g, f)
                yy = lax.rem(y + da * (1 - own) + db * own, 4)
                zz = lax.rem(z + da * own + db * (1 - own), 4)
                base = yy * 4 + zz
                c = (base * 2 + xx) * 2 + rep
                n = counts[0, c]
                p = [pos[s, 0, c] for s in range(3)]
                col = pl.multiple_of((kk * 32 + g * 8 + u * 4 + f) * TILE, TILE)
                for t in range(2):
                    q = t * 2 + u
                    s = jnp.where(p[0] == q, 0, jnp.where(p[1] == q, 1, 2))
                    live = ((p[0] == q) & (n > 0)) | ((p[1] == q) & (n > 1)) | ((p[2] == q) & (n > 2))
                    hi, lo = split(tv[base, xx, s] * jnp.where(live, 1.0, 0.0).astype(F32))
                    ah[t * TILE : (t + 1) * TILE, pl.ds(col, TILE)] = hi
                    al[t * TILE : (t + 1) * TILE, pl.ds(col, TILE)] = lo
            return carry

        lax.fori_loop(0, 4, one, 0)

    def multiply(kk, db, last=False):
        hi, lo = split(feat[kk, db * 8 : db * 8 + 8].reshape(1024, TILE))
        wside[:, 0:TILE] = hi
        wside[:, TILE : 2 * TILE] = lo
        cols = slice((kk * 16 + db * 4) * 256, (kk * 16 + db * 4 + 4) * 256)
        w = wside[...]
        for rows in (slice(0, TILE), slice(TILE, 2 * TILE)):
            new = acc[rows] + (
                jnp.dot(ah[rows, cols], w, preferred_element_type=F32)
                + jnp.dot(al[rows, cols], w, preferred_element_type=F32)
            )
            if last:
                swap[0, rows] = new[:, 0:TILE] + new[:, TILE : 2 * TILE]
                t = rows.start // TILE
                remote(swap.at[0, pl.ds(t * TILE, TILE)], swap.at[1, pl.ds(t * TILE, TILE)], swap_send,
                       swap_recv.at[t], twin).start()
            else:
                acc[rows] = new

    for m in (0, 2, 1, -1):
        i = half * 4 + (-m % 4)
        remote(feat_hbm.at[half], feat.at[0, i], x_send, f_recv.at[i], over(m)).start()
    first_copies = [pltpu.make_async_copy(feat_hbm.at[u], feat.at[0, u * 4], first_sem.at[u]) for u in range(2)]

    @pl.when(native)
    def _():
        for c in first_copies:
            c.start()
        for m in (2, 1, -1):
            for u in range(2):
                i = unit(u, -m, 0)
                remote(feat_hbm.at[u], feat.at[0, i], n_send, f_recv.at[i], near_in(u, m, 0)).start()
        for c in first_copies:
            c.wait()

    @pl.when(jnp.logical_not(native))
    def _():
        for u in range(2):
            wait_f(u, 0, 0)

    def spread(f):
        for u in range(2):
            if f != 0:
                wait_f(u, f, 0)
            for m in (1, -1):
                i = unit(u, f, -m)
                remote(feat.at[0, unit(u, f, 0)], feat.at[0, i], f_send, f_recv.at[i], near_in(u, 0, m)).start()
            give_f(u, f, 0)

    def pass_on(f):
        for u in range(2):
            i = unit(u, f, 2)
            for q, g, m, sem in ((0, 3, 1, f_recv.at[i]), (1, 1, -1, f2_recv.at[u * 4 + f])):
                wait_f(u, f, g)
                relay = remote(
                    quarter(feat.at[0, unit(u, f, g)], q), quarter(feat.at[0, i], q), f_send, sem, near_in(u, 0, m)
                )
                if f == 2:
                    relay.start()
                else:
                    pl.when(native)(relay.start)
                give_f(u, f, g)

    pair = (at(y, z, 1 - xl, 1 - k), rep)

    def across(f):
        @pl.when(native)
        def _():
            for u in range(2):
                i = unit(u, f, 2)
                for q, sem in ((0, f_recv.at[i]), (1, f2_recv.at[u * 4 + f])):
                    remote(
                        quarter(feat.at[0, unit(u, 2, f)], q), quarter(feat.at[0, i], q), f_send, sem, pair
                    ).start()

    def finish(f):
        for u in range(2):
            i = unit(u, f, 2)
            arrived(quarter(feat.at[0, i], 0), f_recv.at[i])
            arrived(quarter(feat.at[0, i], 1), f2_recv.at[u * 4 + f])
            give_f(u, f, 2)

    def sib_multiply(g):
        for i in range(g * 8, g * 8 + 8):
            arrived(feat.at[1, i], fs_recv.at[i])
        multiply(1, g, g == 2)

    spread(0)
    acc[...] = jnp.zeros_like(acc)
    tile_copy.wait()
    for c in places:
        c.wait()
    prep(0, 0)
    for f in (2, 3, 1):
        spread(f)
        if f == 2:
            across(0)
    prep(1, 0)
    prep(0, 3)
    pass_on(0)
    prep(0, 1)
    multiply(0, 0)
    pass_on(2)
    across(3)
    across(1)
    sib_multiply(0)
    pass_on(3)
    prep(1, 3)
    prep(1, 1)
    pass_on(1)
    multiply(0, 3)
    finish(0)
    multiply(0, 1)
    prep(0, 2)
    finish(2)
    sib_multiply(3)
    prep(1, 2)
    finish(3)
    sib_multiply(1)
    finish(1)
    multiply(0, 2)
    sib_multiply(2)

    for l in loads:
        l.wait()
    w = wt[...]
    for t in range(2):
        rows = slice(t * TILE, t * TILE + TILE)
        arrived(swap.at[1, pl.ds(t * TILE, TILE)], swap_recv.at[t])
        agg = swap[0, rows] + swap[1, rows]
        pre = jnp.dot(agg, w, precision=HIGHEST, preferred_element_type=F32)
        gate = jax.nn.sigmoid(pre)
        outv[rows] = pre * gate
        pg = og[rows] * gate * (1.0 + pre * (1.0 - gate))
        pgrad[rows] = pg
        g_t = lax.dot_general(w, pg, (((1,), (1,)), ((), ())), precision=HIGHEST, preferred_element_type=F32)
        hi, lo = split(g_t)
        gs[0:TILE, rows] = hi
        gs[TILE : 2 * TILE, rows] = lo

    def back(kk, g):
        cols = slice((kk * 4 + g) * 1024, (kk * 4 + g + 1) * 1024)
        main = jnp.dot(gs[...], ah[:, cols], preferred_element_type=F32)
        rest = jnp.dot(gs[0:TILE], al[:, cols], preferred_element_type=F32)
        total = main[0:TILE] + main[TILE : 2 * TILE] + rest
        for i in range(8):
            part[kk, g * 8 + i] = total[:, i * TILE : i * TILE + TILE]

    def give_q(g):
        for f in (2, 1, 3, 0):
            for u in range(2):
                i = unit(u, f, g)
                remote(part.at[1, i], sibq.at[i], q_send, q_recv.at[i], sibling).start()

    def take_q(i):
        arrived(sibq.at[i], q_recv.at[i])
        part[0, i] = part[0, i] + sibq[i]

    def step1(u, f):
        i, j = unit(u, f, 2), u * 4 + f
        take_q(i)
        for q, m in ((0, 1), (1, -1)):
            remote(
                quarter(part.at[0, i], q), b_opp.at[q, j], bo_send, bo_recv.at[q, j], near_in(u, 0, m)
            ).start()

    def send_full(u, f, g, q):
        n, j = g // 2, u * 4 + f
        remote(
            quarter(part.at[0, unit(u, f, g)], q), quarter(b_full.at[n, j], q), bf_send, bf_recv.at[n, j, q],
            near_in(u, 0, 1 - 2 * n),
        ).start()

    def step2(u, f, g):
        take_q(unit(u, f, g))
        send_full(u, f, g, 1 - g // 2)

    def step2_sums(u, f):
        for q in range(2):
            g, j = 1 + 2 * q, u * 4 + f
            i, rows = unit(u, f, g), slice(q * 64, q * 64 + 64)
            arrived(b_opp.at[q, j], bo_recv.at[q, j])
            part[0, i, rows] = part[0, i, rows] + b_opp[q, j]
            send_full(u, f, g, q)

    def step3(u, f):
        i, j = unit(u, f, 0), u * 4 + f
        take_q(i)
        for n in range(2):
            for q in range(2):
                arrived(quarter(b_full.at[n, j], q), bf_recv.at[n, j, q])
        part[0, i] = part[0, i] + (b_full[0, j] + b_full[1, j])

    def send_a(u, f, n, m):
        remote(part.at[0, unit(u, f, 0)], a_full.at[n, u], af_send, af_recv.at[n, u], near_in(u, m, 0)).start()

    def weight_term():
        agg_t[...] = (swap[0] + swap[1]).T
        rows = agg_t[pl.ds(pl.multiple_of(rep * 64, 64), 64), :]
        term = jnp.dot(rows, pgrad[...], precision=HIGHEST, preferred_element_type=F32)
        for i in range(8):
            for j in range(2):
                wg[i * 2 + j] = term[i * 8 : i * 8 + 8, j * TILE : j * TILE + TILE]
        for dy, dz in plane_peers:
            there = lax.rem(y + dy, 4) * 4 + lax.rem(z + dz, 4)
            remote(wg.at[there], wr1.at[dy * 4 + dz - 1], w1_send, w1_recv, plane_dev(dy, dz)).start()

    here = y * 4 + z
    line = (rep * 2 + xl) * 2 + k

    def weight_line():
        arrived(wr1, w1_recv)
        total = wg[here]
        for i in range(15):
            total = total + wr1[i]
        wr2[line] = total
        for d in line_peers:
            remote(wr2.at[line], wr2.at[line], w2_send, w2_recv, line_dev(*d)).start()

    def weight_plane():
        arrived(wr2.at[pl.ds(0, 7)], w2_recv)
        for i in range(2):
            total = (wr2[4 * i] + wr2[4 * i + 1]) + (wr2[4 * i + 2] + wr2[4 * i + 3])
            wr3[here, i] = total * (1.0 / math.sqrt(NODES))
        for d in plane_peers:
            remote(wr3.at[here], wr3.at[here], w3_send, w3_recv, plane_dev(*d)).start()

    both = [(u, f) for f in (2, 1, 3, 0) for u in range(2)]
    for g in (2, 1, 3, 0):
        back(1, g)
        give_q(g)
        back(0, g)
        for u, f in both:
            if g == 2:
                step1(u, f)
            elif g != 0:
                step2(u, f, g)
        if g == 3:
            weight_term()
            for u in range(2):
                step2_sums(u, 2)
    for u, f in both[2:]:
        step2_sums(u, f)
    for f, n, m in ((2, 2, 2), (1, 0, 1), (3, 1, -1)):
        for u in range(2):
            step3(u, f)
            send_a(u, f, n, m)
        if f == 2:
            weight_line()
    weight_plane()
    for u in range(2):
        step3(u, 0)

    other = at(y, z, 1 - xl, 1 - k)
    for u in range(2):
        for n in range(3):
            arrived(a_full.at[n, u], af_recv.at[n, u])
        i = unit(u, 0, 0)
        part[0, i] = part[0, i] + (a_full[0, u] + a_full[1, u]) + a_full[2, u]
        total = part.at[0, i]

        @pl.when(native)
        def _():
            remote(total, xr.at[1, u], t_send.at[0], t_recv.at[1, u], twin).start()

        @pl.when(jnp.logical_not(native))
        def _():
            remote(total, xr.at[0, u], t_send.at[0], t_recv.at[0, u], (other, rep)).start()
            remote(total, xr.at[0, u], t_send.at[1], t_recv.at[0, u], (other, 1 - rep)).start()

    for u in range(2):
        arrived(xr.at[0, u], t_recv.at[0, u])

    @pl.when(native)
    def _():
        for u in range(2):
            fgv[u * TILE : (u + 1) * TILE] = (part[0, unit(u, 0, 0)] + xr[0, u]).T
        sent(xr.at[0], t_send.at[0])

    @pl.when(jnp.logical_not(native))
    def _():
        for u in range(2):
            arrived(xr.at[1, u], t_recv.at[1, u])
            fgv[u * TILE : (u + 1) * TILE] = (xr[1, u] + xr[0, u]).T
        sent(xr.at[0], t_send.at[0])
        sent(xr.at[0], t_send.at[1])

    arrived(wr3.at[pl.ds(0, 15)], w3_recv)
    for half_index in range(2):
        for i in range(8):
            for j in range(2):
                wgv[half_index * 64 + i * 8 : half_index * 64 + i * 8 + 8, j * TILE : j * TILE + TILE] = wr3[
                    i * 2 + j, half_index
                ]

    sent(feat.at[0, pl.ds(0, 4)], x_send)

    @pl.when(native)
    def _():
        sent(feat.at[0, pl.ds(0, 6)], n_send)
        sent(feat.at[0, pl.ds(0, 30)], f_send)

    @pl.when(jnp.logical_not(native))
    def _():
        sent(feat.at[0, pl.ds(0, 18)], f_send)

    sent(feat.at[0], fs_send)
    sent(swap.at[0], swap_send)
    sent(part.at[1], q_send)
    sent(b_opp, bo_send)
    sent(b_full, bf_send)
    sent(a_full, af_send)
    sent(wr1, w1_send)
    sent(wr2.at[pl.ds(0, 7)], w2_send)
    sent(wr3.at[pl.ds(0, 15)], w3_send)


def body(features, weight, tile_values, tile_pos, tile_counts, out_grad):
    dma = pltpu.SemaphoreType.DMA
    vm = pltpu.VMEM
    any_space = pl.BlockSpec(memory_space=pl.ANY)
    vspace = pl.BlockSpec(memory_space=pltpu.VMEM)
    shapes = (
        jax.ShapeDtypeStruct((256, 256), F32),
        jax.ShapeDtypeStruct((256, 128), F32),
        jax.ShapeDtypeStruct((128, 256), F32),
    )
    return pl.pallas_call(
        kernel,
        out_shape=tuple(pltpu.VMEM(x.shape, x.dtype) for x in shapes),
        in_specs=[any_space] * 6,
        out_specs=(vspace,) * 3,
        scratch_shapes=[
            pltpu.SMEM((3, 1, 64), jnp.int32),
            pltpu.SMEM((1, 64), jnp.int32),
            vm((16, 2, 3, TILE, TILE), F32),
            vm((256, 8192), BF16),
            vm((256, 8192), BF16),
            vm((2, 32, TILE, TILE), F32),
            vm((1024, 256), BF16),
            vm((256, 256), F32),
            vm((2, 256, TILE), F32),
            vm((TILE, 256), F32),
            vm((TILE, 256), F32),
            vm((256, 256), F32),
            vm((256, 256), F32),
            vm((256, 256), BF16),
            vm((2, 32, TILE, TILE), F32),
            vm((32, TILE, TILE), F32),
            vm((2, 8, 64, TILE), F32),
            vm((2, 8, TILE, TILE), F32),
            vm((3, 2, TILE, TILE), F32),
            vm((2, 2, TILE, TILE), F32),
            vm((16, 8, TILE), F32),
            vm((15, 8, TILE), F32),
            vm((8, 8, TILE), F32),
            vm((16, 2, 8, TILE), F32),
            dma, dma((4,)), dma((2,)),
            dma, dma((32,)), dma((8,)), dma, dma((32,)), dma, dma, dma, dma((2,)),
            dma, dma((32,)), dma, dma((2, 8)), dma, dma((2, 8, 2)), dma, dma((3, 2)),
            dma((2,)), dma((2, 2)), dma, dma, dma, dma, dma, dma,
        ],
        compiler_params=pltpu.CompilerParams(
            collective_id=0, has_side_effects=True, vmem_limit_bytes=60 * 1024 * 1024
        ),
        cost_estimate=pl.CostEstimate(flops=3_000_000_000, bytes_accessed=8_000_000, transcendentals=65536),
    )(
        features.reshape(2, TILE, TILE),
        weight,
        tile_values.reshape(16, 2, 2, 3, TILE, TILE),
        tile_pos.transpose(2, 0, 1),
        tile_counts,
        out_grad,
    )


def solution(mesh):
    return jax.shard_map(
        body,
        mesh=mesh,
        in_specs=(
            P("blk", None),
            P(),
            P("blk", None, None, None, None),
            P("blk", None, None),
            P("blk", None),
            P("blk", None),
        ),
        out_specs=(P("blk", None), P("blk", None), P()),
        check_vma=False,
    )
```

```python
import math

import jax
import jax.numpy as jnp
from jax import lax
from jax.experimental import pallas as pl
from jax.experimental.pallas import tpu as pltpu
from jax.sharding import PartitionSpec as P

HIGHEST = lax.Precision.HIGHEST
MESH = pl.DeviceIdType.MESH
F32, BF16 = jnp.float32, jnp.bfloat16
NODES = 16384
TILE = 128


def split(x):
    hi = x.astype(BF16)
    return hi, (x - hi.astype(F32)).astype(BF16)


def kernel(
    feat_hbm, weight_hbm, tiles_hbm, pos_hbm, counts_hbm, ograd_hbm,
    outv, fgv, wgv,
    pos, counts, tv, ah, al, feat, wside, acc, swap, agg_t, wt, og, pgrad, gs,
    part, sibq, b_opp, b_full, a_full, xr,
    wg, wr1, wr2, wr3,
    tile_sem, load_sem, first_sem,
    f_send, f_recv, f2_recv, fs_send, fs_recv, x_send, n_send, swap_send, swap_recv,
    q_send, q_recv, bo_send, bo_recv, bf_send, bf_recv, af_send, af_recv,
    t_send, t_recv, w1_send, w1_recv, w2_send, w2_recv, w3_send, w3_recv,
):
    blk, rep = lax.axis_index("blk"), lax.axis_index("rep")
    y, z = lax.rem(lax.div(blk, 16), 4), lax.rem(lax.div(blk, 4), 4)
    xl, k = lax.rem(lax.div(blk, 2), 2), lax.rem(blk, 2)
    native = k == rep

    def at(yy, zz, xx, kk):
        return ((lax.rem(yy + 8, 4) * 4 + lax.rem(zz + 8, 4)) * 2 + xx) * 2 + kk

    def near(da, db):
        return (at(y + da * (1 - k) + db * k, z + da * k + db * (1 - k), xl, k), rep)

    sibling = (at(y, z, xl, 1 - k), rep)

    def remote(src, dst, ssem, rsem, dev):
        return pltpu.make_async_remote_copy(
            src_ref=src, dst_ref=dst, send_sem=ssem, recv_sem=rsem, device_id=dev, device_id_type=MESH
        )

    def arrived(dst, rsem):
        remote(dst, dst, rsem, rsem, sibling).wait_recv()

    def sent(src, ssem):
        remote(src, src, ssem, ssem, sibling).wait_send()

    tile_copy = pltpu.make_async_copy(tiles_hbm.at[:, :, rep], tv, tile_sem)
    tile_copy.start()
    loads = [
        pltpu.make_async_copy(weight_hbm, wt, load_sem.at[0]),
        pltpu.make_async_copy(ograd_hbm, og, load_sem.at[1]),
    ]
    places = [
        pltpu.make_async_copy(pos_hbm, pos, load_sem.at[2]),
        pltpu.make_async_copy(counts_hbm, counts, load_sem.at[3]),
    ]
    for c in places + loads:
        c.start()

    barrier = pltpu.get_barrier_semaphore()
    plane_peers = [(dy, dz) for dy in range(4) for dz in range(4) if (dy, dz) != (0, 0)]
    line_peers = [(i, j, l) for i in range(2) for j in range(2) for l in range(2) if (i, j, l) != (0, 0, 0)]

    def plane_dev(dy, dz):
        return (at(y + dy, z + dz, xl, k), rep)

    def line_dev(i, j, l):
        return (at(y, z, lax.rem(xl + j, 2), lax.rem(k + l, 2)), lax.rem(rep + i, 2))

    def near_in(u, mf, mg):
        return near(mf, mg) if u == 0 else near(mg, mf)

    half = lax.rem(k + rep, 2)
    along_y = k * (1 - half) + (1 - k) * half

    def over(m):
        return (at(y + m * along_y, z + m * (1 - along_y), 1 - xl, 1 - k), k)

    def over_from(m, i):
        u = lax.rem(1 - k + i, 2)
        c = (1 - k) * (1 - u) + k * u
        return (at(y + m * c, z + m * (1 - c), 1 - xl, 1 - k), i)

    def greet(dev):
        pl.semaphore_signal(barrier, inc=1, device_id=dev, device_id_type=MESH)

    twin = (blk, 1 - rep)
    peers = [near(2, 0), near(0, 2), twin, near(1, 0), near(-1, 0), near(0, 1), near(0, -1), sibling]
    @pl.when(jnp.logical_not(native))
    def _():
        for m in (2, 1, -1):
            for i in range(2):
                greet(over_from(m, i))

    for i in range(2):
        greet((at(y, z, 1 - xl, 1 - k), i))
    for d in peers:
        greet(d)
    pl.semaphore_wait(barrier, len(peers) + 2 + 3)

    def unit(u, f, g):
        return g % 4 * 8 + u * 4 + f % 4

    def wait_f(u, f, g):
        i = unit(u, f, g)
        arrived(feat.at[0, i], f_recv.at[i])

    def give_f(u, f, g):
        i = unit(u, f, g)
        remote(feat.at[0, i], feat.at[1, i], fs_send, fs_recv.at[i], sibling).start()

    def quarter(ref, q):
        return ref.at[pl.ds(q * 64, 64)]

    def prep(kk, g):
        own = k if kk == 0 else 1 - k
        xx = lax.rem(xl + own + rep, 2)

        def one(f, carry):
            for u in range(2):
                da, db = (f, g) if u == 0 else (g, f)
                yy = lax.rem(y + da * (1 - own) + db * own, 4)
                zz = lax.rem(z + da * own + db * (1 - own), 4)
                base = yy * 4 + zz
                c = (base * 2 + xx) * 2 + rep
                n = counts[0, c]
                p = [pos[s, 0, c] for s in range(3)]
                col = pl.multiple_of((kk * 32 + g * 8 + u * 4 + f) * TILE, TILE)
                for t in range(2):
                    q = t * 2 + u
                    s = jnp.where(p[0] == q, 0, jnp.where(p[1] == q, 1, 2))
                    live = ((p[0] == q) & (n > 0)) | ((p[1] == q) & (n > 1)) | ((p[2] == q) & (n > 2))
                    hi, lo = split(tv[base, xx, s] * jnp.where(live, 1.0, 0.0).astype(F32))
                    ah[t * TILE : (t + 1) * TILE, pl.ds(col, TILE)] = hi
                    al[t * TILE : (t + 1) * TILE, pl.ds(col, TILE)] = lo
            return carry

        lax.fori_loop(0, 4, one, 0)

    def multiply(kk, db, last=False):
        hi, lo = split(feat[kk, db * 8 : db * 8 + 8].reshape(1024, TILE))
        wside[:, 0:TILE] = hi
        wside[:, TILE : 2 * TILE] = lo
        cols = slice((kk * 16 + db * 4) * 256, (kk * 16 + db * 4 + 4) * 256)
        w = wside[...]
        for rows in (slice(0, TILE), slice(TILE, 2 * TILE)):
            new = acc[rows] + (
                jnp.dot(ah[rows, cols], w, preferred_element_type=F32)
                + jnp.dot(al[rows, cols], w, preferred_element_type=F32)
            )
            if last:
                swap[0, rows] = new[:, 0:TILE] + new[:, TILE : 2 * TILE]
                t = rows.start // TILE
                remote(swap.at[0, pl.ds(t * TILE, TILE)], swap.at[1, pl.ds(t * TILE, TILE)], swap_send,
                       swap_recv.at[t], twin).start()
            else:
                acc[rows] = new

    def spread_from(source, u, f):
        for m in (1, -1):
            i = unit(u, f, -m)
            remote(source, feat.at[0, i], f_send, f_recv.at[i], near_in(u, 0, m)).start()
        i = unit(u, f, 0)
        remote(source, feat.at[1, i], fs_send, fs_recv.at[i], sibling).start()

    for m in (0, 2, 1, -1):
        i = half * 4 + (-m % 4)
        remote(feat_hbm.at[half], feat.at[0, i], x_send, f_recv.at[i], over(m)).start()
    first_copies = [pltpu.make_async_copy(feat_hbm.at[u], feat.at[0, u * 4], first_sem.at[u]) for u in range(2)]

    @pl.when(native)
    def _():
        for c in first_copies:
            c.start()
        for m in (2, 1, -1):
            for u in range(2):
                i = unit(u, -m, 0)
                remote(feat_hbm.at[u], feat.at[0, i], n_send, f_recv.at[i], near_in(u, m, 0)).start()
        for u in range(2):
            spread_from(feat_hbm.at[u], u, 0)

    @pl.when(jnp.logical_not(native))
    def _():
        for u in range(2):
            wait_f(u, 0, 0)
            spread_from(feat.at[0, unit(u, 0, 0)], u, 0)

    def spread(f):
        for u in range(2):
            wait_f(u, f, 0)
            spread_from(feat.at[0, unit(u, f, 0)], u, f)

    def pass_on(f):
        for u in range(2):
            i = unit(u, f, 2)
            for q, g, m, sem in ((0, 3, 1, f_recv.at[i]), (1, 1, -1, f2_recv.at[u * 4 + f])):
                wait_f(u, f, g)
                relay = remote(
                    quarter(feat.at[0, unit(u, f, g)], q), quarter(feat.at[0, i], q), f_send, sem, near_in(u, 0, m)
                )
                if f == 2:
                    relay.start()
                else:
                    pl.when(native)(relay.start)
                give_f(u, f, g)

    pair = (at(y, z, 1 - xl, 1 - k), rep)

    def across(f):
        @pl.when(native)
        def _():
            for u in range(2):
                i = unit(u, f, 2)
                for q, sem in ((0, f_recv.at[i]), (1, f2_recv.at[u * 4 + f])):
                    remote(
                        quarter(feat.at[0, unit(u, 2, f)], q), quarter(feat.at[0, i], q), f_send, sem, pair
                    ).start()

    def finish(f):
        for u in range(2):
            i = unit(u, f, 2)
            arrived(quarter(feat.at[0, i], 0), f_recv.at[i])
            arrived(quarter(feat.at[0, i], 1), f2_recv.at[u * 4 + f])
            give_f(u, f, 2)

    def sib_multiply(g):
        for i in range(g * 8, g * 8 + 8):
            arrived(feat.at[1, i], fs_recv.at[i])
        multiply(1, g, g == 2)

    acc[...] = jnp.zeros_like(acc)
    tile_copy.wait()
    for c in places:
        c.wait()
    prep(0, 0)
    for f in (2, 3, 1):
        spread(f)
        if f == 2:
            across(0)
    prep(1, 0)
    prep(0, 3)
    pass_on(0)
    prep(0, 1)

    @pl.when(native)
    def _():
        for c in first_copies:
            c.wait()

    multiply(0, 0)
    pass_on(2)
    across(3)
    across(1)
    sib_multiply(0)
    pass_on(3)
    prep(1, 3)
    prep(1, 1)
    pass_on(1)
    multiply(0, 3)
    finish(0)
    multiply(0, 1)
    prep(0, 2)
    finish(2)
    sib_multiply(3)
    prep(1, 2)
    finish(3)
    sib_multiply(1)
    finish(1)
    multiply(0, 2)
    sib_multiply(2)

    for l in loads:
        l.wait()
    w = wt[...]
    for t in range(2):
        rows = slice(t * TILE, t * TILE + TILE)
        arrived(swap.at[1, pl.ds(t * TILE, TILE)], swap_recv.at[t])
        agg = swap[0, rows] + swap[1, rows]
        pre = jnp.dot(agg, w, precision=HIGHEST, preferred_element_type=F32)
        gate = jax.nn.sigmoid(pre)
        outv[rows] = pre * gate
        pg = og[rows] * gate * (1.0 + pre * (1.0 - gate))
        pgrad[rows] = pg
        g_t = lax.dot_general(w, pg, (((1,), (1,)), ((), ())), precision=HIGHEST, preferred_element_type=F32)
        hi, lo = split(g_t)
        gs[0:TILE, rows] = hi
        gs[TILE : 2 * TILE, rows] = lo

    def back(kk, g):
        cols = slice((kk * 4 + g) * 1024, (kk * 4 + g + 1) * 1024)
        main = jnp.dot(gs[...], ah[:, cols], preferred_element_type=F32)
        rest = jnp.dot(gs[0:TILE], al[:, cols], preferred_element_type=F32)
        total = main[0:TILE] + main[TILE : 2 * TILE] + rest
        for i in range(8):
            part[kk, g * 8 + i] = total[:, i * TILE : i * TILE + TILE]

    def give_q(g):
        for f in (2, 1, 3, 0):
            for u in range(2):
                i = unit(u, f, g)
                remote(part.at[1, i], sibq.at[i], q_send, q_recv.at[i], sibling).start()

    def take_q(i):
        arrived(sibq.at[i], q_recv.at[i])
        part[0, i] = part[0, i] + sibq[i]

    def step1(u, f):
        i, j = unit(u, f, 2), u * 4 + f
        take_q(i)
        for q, m in ((0, 1), (1, -1)):
            remote(
                quarter(part.at[0, i], q), b_opp.at[q, j], bo_send, bo_recv.at[q, j], near_in(u, 0, m)
            ).start()

    def send_full(u, f, g, q):
        n, j = g // 2, u * 4 + f
        remote(
            quarter(part.at[0, unit(u, f, g)], q), quarter(b_full.at[n, j], q), bf_send, bf_recv.at[n, j, q],
            near_in(u, 0, 1 - 2 * n),
        ).start()

    def step2(u, f, g):
        take_q(unit(u, f, g))
        send_full(u, f, g, 1 - g // 2)

    def step2_sums(u, f):
        for q in range(2):
            g, j = 1 + 2 * q, u * 4 + f
            i, rows = unit(u, f, g), slice(q * 64, q * 64 + 64)
            arrived(b_opp.at[q, j], bo_recv.at[q, j])
            part[0, i, rows] = part[0, i, rows] + b_opp[q, j]
            send_full(u, f, g, q)

    def step3(u, f):
        i, j = unit(u, f, 0), u * 4 + f
        take_q(i)
        for n in range(2):
            for q in range(2):
                arrived(quarter(b_full.at[n, j], q), bf_recv.at[n, j, q])
        part[0, i] = part[0, i] + (b_full[0, j] + b_full[1, j])

    def send_a(u, f, n, m):
        remote(part.at[0, unit(u, f, 0)], a_full.at[n, u], af_send, af_recv.at[n, u], near_in(u, m, 0)).start()

    def weight_term():
        agg_t[...] = (swap[0] + swap[1]).T
        rows = agg_t[pl.ds(pl.multiple_of(rep * 64, 64), 64), :]
        term = jnp.dot(rows, pgrad[...], precision=HIGHEST, preferred_element_type=F32)
        for i in range(8):
            for j in range(2):
                wg[i * 2 + j] = term[i * 8 : i * 8 + 8, j * TILE : j * TILE + TILE]
        for dy, dz in plane_peers:
            there = lax.rem(y + dy, 4) * 4 + lax.rem(z + dz, 4)
            remote(wg.at[there], wr1.at[dy * 4 + dz - 1], w1_send, w1_recv, plane_dev(dy, dz)).start()

    here = y * 4 + z
    line = (rep * 2 + xl) * 2 + k

    def weight_line():
        arrived(wr1, w1_recv)
        total = wg[here]
        for i in range(15):
            total = total + wr1[i]
        wr2[line] = total
        for d in line_peers:
            remote(wr2.at[line], wr2.at[line], w2_send, w2_recv, line_dev(*d)).start()

    def weight_plane():
        arrived(wr2.at[pl.ds(0, 7)], w2_recv)
        for i in range(2):
            total = (wr2[4 * i] + wr2[4 * i + 1]) + (wr2[4 * i + 2] + wr2[4 * i + 3])
            wr3[here, i] = total * (1.0 / math.sqrt(NODES))
        for d in plane_peers:
            remote(wr3.at[here], wr3.at[here], w3_send, w3_recv, plane_dev(*d)).start()

    both = [(u, f) for f in (2, 1, 3, 0) for u in range(2)]
    for g in (2, 1, 3, 0):
        back(1, g)
        give_q(g)
        back(0, g)
        for u, f in both:
            if g == 2:
                step1(u, f)
            elif g != 0:
                step2(u, f, g)
        if g == 3:
            weight_term()
            for u in range(2):
                step2_sums(u, 2)
    for u, f in both[2:]:
        step2_sums(u, f)
    for f, n, m in ((2, 2, 2), (1, 0, 1), (3, 1, -1)):
        for u in range(2):
            step3(u, f)
            send_a(u, f, n, m)
        if f == 2:
            weight_line()
    weight_plane()
    for u in range(2):
        step3(u, 0)

    other = at(y, z, 1 - xl, 1 - k)
    for u in range(2):
        for n in range(3):
            arrived(a_full.at[n, u], af_recv.at[n, u])
        i = unit(u, 0, 0)
        part[0, i] = part[0, i] + (a_full[0, u] + a_full[1, u]) + a_full[2, u]
        total = part.at[0, i]

        @pl.when(native)
        def _():
            remote(total, xr.at[1, u], t_send.at[0], t_recv.at[1, u], twin).start()

        @pl.when(jnp.logical_not(native))
        def _():
            remote(total, xr.at[0, u], t_send.at[0], t_recv.at[0, u], (other, rep)).start()
            remote(total, xr.at[0, u], t_send.at[1], t_recv.at[0, u], (other, 1 - rep)).start()

    for u in range(2):
        arrived(xr.at[0, u], t_recv.at[0, u])

    @pl.when(native)
    def _():
        for u in range(2):
            fgv[u * TILE : (u + 1) * TILE] = (part[0, unit(u, 0, 0)] + xr[0, u]).T
        sent(xr.at[0], t_send.at[0])

    @pl.when(jnp.logical_not(native))
    def _():
        for u in range(2):
            arrived(xr.at[1, u], t_recv.at[1, u])
            fgv[u * TILE : (u + 1) * TILE] = (xr[1, u] + xr[0, u]).T
        sent(xr.at[0], t_send.at[0])
        sent(xr.at[0], t_send.at[1])

    arrived(wr3.at[pl.ds(0, 15)], w3_recv)
    for half_index in range(2):
        for i in range(8):
            for j in range(2):
                wgv[half_index * 64 + i * 8 : half_index * 64 + i * 8 + 8, j * TILE : j * TILE + TILE] = wr3[
                    i * 2 + j, half_index
                ]

    sent(feat.at[0, pl.ds(0, 4)], x_send)

    @pl.when(native)
    def _():
        sent(feat.at[0, pl.ds(0, 6)], n_send)
        sent(feat.at[0, pl.ds(0, 30)], f_send)

    @pl.when(jnp.logical_not(native))
    def _():
        sent(feat.at[0, pl.ds(0, 18)], f_send)

    sent(feat.at[0], fs_send)
    sent(swap.at[0], swap_send)
    sent(part.at[1], q_send)
    sent(b_opp, bo_send)
    sent(b_full, bf_send)
    sent(a_full, af_send)
    sent(wr1, w1_send)
    sent(wr2.at[pl.ds(0, 7)], w2_send)
    sent(wr3.at[pl.ds(0, 15)], w3_send)


def body(features, weight, tile_values, tile_pos, tile_counts, out_grad):
    dma = pltpu.SemaphoreType.DMA
    vm = pltpu.VMEM
    any_space = pl.BlockSpec(memory_space=pl.ANY)
    vspace = pl.BlockSpec(memory_space=pltpu.VMEM)
    shapes = (
        jax.ShapeDtypeStruct((256, 256), F32),
        jax.ShapeDtypeStruct((256, 128), F32),
        jax.ShapeDtypeStruct((128, 256), F32),
    )
    return pl.pallas_call(
        kernel,
        out_shape=tuple(pltpu.VMEM(x.shape, x.dtype) for x in shapes),
        in_specs=[any_space] * 6,
        out_specs=(vspace,) * 3,
        scratch_shapes=[
            pltpu.SMEM((3, 1, 64), jnp.int32),
            pltpu.SMEM((1, 64), jnp.int32),
            vm((16, 2, 3, TILE, TILE), F32),
            vm((256, 8192), BF16),
            vm((256, 8192), BF16),
            vm((2, 32, TILE, TILE), F32),
            vm((1024, 256), BF16),
            vm((256, 256), F32),
            vm((2, 256, TILE), F32),
            vm((TILE, 256), F32),
            vm((TILE, 256), F32),
            vm((256, 256), F32),
            vm((256, 256), F32),
            vm((256, 256), BF16),
            vm((2, 32, TILE, TILE), F32),
            vm((32, TILE, TILE), F32),
            vm((2, 8, 64, TILE), F32),
            vm((2, 8, TILE, TILE), F32),
            vm((3, 2, TILE, TILE), F32),
            vm((2, 2, TILE, TILE), F32),
            vm((16, 8, TILE), F32),
            vm((15, 8, TILE), F32),
            vm((8, 8, TILE), F32),
            vm((16, 2, 8, TILE), F32),
            dma, dma((4,)), dma((2,)),
            dma, dma((32,)), dma((8,)), dma, dma((32,)), dma, dma, dma, dma((2,)),
            dma, dma((32,)), dma, dma((2, 8)), dma, dma((2, 8, 2)), dma, dma((3, 2)),
            dma((2,)), dma((2, 2)), dma, dma, dma, dma, dma, dma,
        ],
        compiler_params=pltpu.CompilerParams(
            collective_id=0, has_side_effects=True, vmem_limit_bytes=60 * 1024 * 1024
        ),
        cost_estimate=pl.CostEstimate(flops=3_000_000_000, bytes_accessed=8_000_000, transcendentals=65536),
    )(
        features.reshape(2, TILE, TILE),
        weight,
        tile_values.reshape(16, 2, 2, 3, TILE, TILE),
        tile_pos.transpose(2, 0, 1),
        tile_counts,
        out_grad,
    )


def solution(mesh):
    return jax.shard_map(
        body,
        mesh=mesh,
        in_specs=(
            P("blk", None),
            P(),
            P("blk", None, None, None, None),
            P("blk", None, None),
            P("blk", None),
            P("blk", None),
        ),
        out_specs=(P("blk", None), P("blk", None), P()),
        check_vma=False,
    )
```
